512 devices in a mesh: ctx: 64 (over z_lo, y, x), work: 8 (over z_hi, core).
Axes of the slice: x: 4, y: 8, z: 8 (z_hi: 4, z_lo: 2; z = z_hi * 2 + z_lo), core: 2. Of those that a mesh axis runs over, the one named last changes fastest.
Arguments:
- inputs: bfloat16 [8, 16384, 2880], P('work', 'ctx'), may hold values from -6 to 6
- queries: bfloat16 [8, 16384, 2048], P('work', 'ctx')
- keys: bfloat16 [8, 16384, 256], P('work', 'ctx')
- out_grad: bfloat16 [8, 16384, 2048], P('work', 'ctx'), may hold values from -6 to 6
- positions: int32 [8, 16384], P('work', 'ctx'), may hold values from 0 to 16383, as said below
- bands: int32 [32], replicated, may hold values from 32 to 128, as said below
- step: int32 [1], replicated, may hold values from 1 to 16
- value_weight: float32 [8, 2880, 256], P('work', 'ctx'), may hold values from -0.109375 to 0.109375
- moment_one: float32 [8, 2880, 256], P('work', 'ctx'), may hold values from -0.0078125 to 0.0078125
- moment_two: float32 [8, 2880, 256], P('work', 'ctx'), may hold values from 1e-08 to 1e-06
Outputs:
- attn_out: bfloat16 [8, 16384, 2048], P('work', 'ctx')
- mean_weight: float32 [2880, 256], P('ctx')
- mean_one: float32 [2880, 256], P('ctx')
- mean_two: float32 [2880, 256], P('ctx')
The draws below stay inside these ranges and needn't reach their ends.
Inputs may be any that keep to these rules, and one draw needn't show every extreme that they name: `positions`: in each worker's sequence a token's position is 0 at the first token and at each document start, else one more than the previous token's. One worker's sequence is a single document. `bands`: one head has exactly 128.
All inputs are finite; a program needn't handle non-finite values.
Results may differ from the reference program's by a relative error of at most 0.0015.
The reference program's roundings to bfloat16 on the way count: a program that leaves them out, or rounds other values in their place, can miss the bound.
Values may be sent and summed in bfloat16 or wider, within the bound.
A program may use at most 64 MiB of HBM per device.

```python
import math
import jax
import jax.numpy as jnp
from jax import lax

D = 2880
HD = 64
QH = 32
KH = 4
LOOKBACK_SPAN = 128
TOKENS_PER_UNIT = 256
TOKENS = 16384
WORKERS = 8
N_CTX = 64
N_WORK = 8


def shared_keys(key):
    return jax.random.normal(jax.random.fold_in(key, 7), (WORKERS, TOKENS, KH * HD), jnp.float32)


def draw_keys(key, part):
    return shared_keys(key).astype(jnp.bfloat16)


def draw_queries(key, part):
    base = jax.random.normal(jax.random.fold_in(key, 13), (WORKERS, TOKENS, QH * HD), jnp.float32)
    return base.astype(jnp.bfloat16)


def draw_positions(key, part):
    index = jnp.broadcast_to(jnp.arange(TOKENS, dtype=jnp.int32), (WORKERS, TOKENS))
    worker = jnp.broadcast_to(jnp.arange(WORKERS, dtype=jnp.int32)[:, None], (WORKERS, TOKENS))
    single = jax.random.randint(jax.random.fold_in(key, 37), (), 0, WORKERS)
    starts = jax.random.randint(jax.random.fold_in(key, 23), (WORKERS, TOKENS), 0, 2 * TOKENS_PER_UNIT) == 0
    starts = starts & (worker != single) | (index == 0)
    begun = jax.lax.cummax(jnp.where(starts, index, 0), axis=1)
    return (index - begun).astype(jnp.int32)


def draw_bands(key, part):
    widths = jax.random.randint(jax.random.fold_in(key, 29), (QH,), LOOKBACK_SPAN // 4, LOOKBACK_SPAN + 1)
    chosen = jax.random.randint(jax.random.fold_in(key, 31), (1,), 0, QH)
    return jnp.where(jnp.arange(QH, dtype=jnp.int32) == chosen, LOOKBACK_SPAN, widths).astype(jnp.int32)


def levels(rng, extent, cuts, least, top_value):
    factor_of = 1.0
    for position, blocks in cuts:
        draws = jax.random.uniform(jax.random.fold_in(jax.random.fold_in(rng, 6), position), (blocks,), jnp.float32, least / len(cuts), top_value / len(cuts))
        factor_of = factor_of * jnp.repeat(jnp.exp(draws), extent[position] // blocks).reshape((-1,) + (1,) * (len(extent) - 1 - position))
    return factor_of


def gaussian(key, extent, spread, reach, shards=(), held_as=jnp.bfloat16):
    loudness = levels(key, extent, shards, -0.22, 0.18) if shards else 1.0
    entries = jax.random.normal(key, extent, jnp.float32) * spread * loudness
    return jnp.minimum(jnp.maximum(entries, -reach), reach).astype(held_as)


def setup_inputs(seed: int = 0) -> dict:
    arg_keys = jax.random.split(jax.random.key(seed), 11)
    inputs = gaussian(arg_keys[0], (WORKERS, TOKENS, D), 1.0, 6.0, ((0, 8), (1, 64)))
    queries = draw_queries(jax.random.fold_in(arg_keys[10], 71), 0)
    keys = draw_keys(jax.random.fold_in(arg_keys[10], 71), 0)
    out_grad = gaussian(arg_keys[3], (WORKERS, TOKENS, QH * HD), 1.0, 6.0, ((0, 8), (1, 64)))
    positions = draw_positions(jax.random.fold_in(arg_keys[10], 71), 0)
    bands = draw_bands(jax.random.fold_in(arg_keys[10], 71), 0)
    step = jax.random.randint(arg_keys[6], (1,), 1, 17).astype(jnp.int32)
    value_weight = gaussian(arg_keys[7], (WORKERS, D, KH * HD), D ** -0.5, 0.109375, ((0, 8), (1, 64)), jnp.float32)
    moment_one = gaussian(arg_keys[8], (WORKERS, D, KH * HD), 0.0005, 0.0078125, ((0, 8), (1, 64)), jnp.float32)
    moment_two = jnp.clip(jnp.exp(math.log(9.999999974752427e-07) - 4.6051702 * jax.random.uniform(arg_keys[9], (WORKERS, D, KH * HD), jnp.float32) ** levels(arg_keys[9], (WORKERS, D, KH * HD), ((0, 8), (1, 64)), -0.2, 0.2)), 9.99999993922529e-09, 9.999999974752427e-07)
    return dict(inputs=inputs, queries=queries, keys=keys, out_grad=out_grad, positions=positions, bands=bands, step=step, value_weight=value_weight, moment_one=moment_one, moment_two=moment_two)


beta_one = 0.9
beta_two = 0.95
adam_eps = 1e-08
learn_rate = 0.01
clip_norm = 0.5

def attend(qrows, krows, vrows, grows, bands, pos):
    count = qrows.shape[0]
    span = krows.shape[0]
    halo = span - count
    group = QH // KH
    dist = lax.broadcasted_iota(jnp.int32, (count, span), 0) + halo - lax.broadcasted_iota(jnp.int32, (count, span), 1)
    near = (dist >= 0) & (dist <= pos[:, None])
    outputs = []
    grads = []
    for head in range(KH):
        lo = head * group * HD
        hi = (head + 1) * group * HD
        query = qrows[:, lo:hi].reshape(count, group, HD).astype(jnp.float32)
        keyed = krows[:, head * HD:(head + 1) * HD].astype(jnp.float32)
        valued = vrows[:, head * HD:(head + 1) * HD].astype(jnp.float32)
        cotan = grows[:, lo:hi].reshape(count, group, HD).astype(jnp.float32)
        limit = bands[head * group:(head + 1) * group]
        allowed = near[None] & (dist[None] <= limit[:, None, None])
        scores = jnp.einsum('qgd,kd->gqk', query, keyed) * HD ** (-0.5)
        scores = jnp.where(allowed, scores, -1e+30)
        top = lax.optimization_barrier(jnp.max(scores, axis=2, keepdims=True))
        expo = jnp.exp(scores - top)
        probs = (expo / lax.optimization_barrier(jnp.sum(expo, axis=2, keepdims=True))).astype(jnp.bfloat16).astype(jnp.float32)
        outputs.append(jnp.einsum('gqk,kd->qgd', probs, valued).reshape(count, group * HD))
        grads.append(jnp.einsum('gqk,qgd->kd', probs, cotan))
    return (jnp.concatenate(outputs, 1).astype(jnp.bfloat16), jnp.concatenate(grads, 1))

def reference(inputs, queries, keys, out_grad, positions, bands, step, value_weight, moment_one, moment_two):
    window_extent = KH * HD

    def one_worker(items):
        acts, query, keyed, cotan, pos, weight, first, second = items
        value_vectors = jnp.dot(acts, weight.astype(jnp.bfloat16), preferred_element_type=jnp.float32).astype(jnp.bfloat16)
        kpad = jnp.concatenate([jnp.zeros((LOOKBACK_SPAN, window_extent), jnp.bfloat16), keyed], 0)
        value_padded = jnp.concatenate([jnp.zeros((LOOKBACK_SPAN, window_extent), jnp.bfloat16), value_vectors], 0)

        def block(dv_pad, index):
            begin_offset = (index * TOKENS_PER_UNIT).astype(jnp.int32)
            qb = lax.dynamic_slice_in_dim(query, begin_offset, TOKENS_PER_UNIT, 0)
            gb = lax.dynamic_slice_in_dim(cotan, begin_offset, TOKENS_PER_UNIT, 0)
            pb = lax.dynamic_slice_in_dim(pos, begin_offset, TOKENS_PER_UNIT, 0)
            kb = lax.dynamic_slice_in_dim(kpad, begin_offset, TOKENS_PER_UNIT + LOOKBACK_SPAN, 0)
            value_band_rows = lax.dynamic_slice_in_dim(value_padded, begin_offset, TOKENS_PER_UNIT + LOOKBACK_SPAN, 0)
            out, grad_block = attend(qb, kb, value_band_rows, gb, bands, pb)
            current = lax.dynamic_slice_in_dim(dv_pad, begin_offset, TOKENS_PER_UNIT + LOOKBACK_SPAN, 0)
            dv_pad = lax.dynamic_update_slice_in_dim(dv_pad, current + grad_block, begin_offset, 0)
            return (dv_pad, out)
        dv_pad, outs = lax.scan(block, jnp.zeros((TOKENS + LOOKBACK_SPAN, window_extent), jnp.float32), jnp.arange(N_CTX, dtype=jnp.int32))
        value_grad = dv_pad[LOOKBACK_SPAN:].astype(jnp.bfloat16)
        grad = jnp.dot(acts.T, value_grad, preferred_element_type=jnp.float32) / TOKENS
        norm = jnp.sqrt(jnp.sum(grad * grad))
        grad = grad * jnp.minimum(1.0, clip_norm / (norm + 1e-06))
        first = beta_one * first + (1.0 - beta_one) * grad
        second = beta_two * second + (1.0 - beta_two) * grad * grad
        count = step[0].astype(jnp.float32)
        fix_one = 1.0 - jnp.power(jnp.float32(beta_one), count)
        fix_two = 1.0 - jnp.power(jnp.float32(beta_two), count)
        weight = weight - learn_rate * (first / fix_one) / (jnp.sqrt(second / fix_two) + adam_eps)
        return (outs.reshape(TOKENS, QH * HD), weight, first, second)
    outs, weights, firsts, seconds = lax.map(one_worker, (inputs, queries, keys, out_grad, positions, value_weight, moment_one, moment_two))
    return (outs, lax.optimization_barrier(jnp.sum(weights, axis=0)) / N_WORK, lax.optimization_barrier(jnp.sum(firsts, axis=0)) / N_WORK, lax.optimization_barrier(jnp.sum(seconds, axis=0)) / N_WORK)
```

```python
import functools
import math

import jax
import jax.numpy as jnp
import numpy as np
from jax import lax
from jax.experimental import pallas as pl
from jax.experimental.pallas import tpu as pltpu
from jax.sharding import PartitionSpec as P

D = 2880
HD = 64
QH = 32
KH = 4
SPAN = 128
ROWS = 256
NZ, NY, NX = 2, 8, 4
NCTX = NZ * NY * NX
NH = 4
NW = 8
OWN = D // NCTX
PAD = 48
TILES = NCTX * PAD // 128

beta_one = 0.9
beta_two = 0.95
adam_eps = 1e-08
learn_rate = 0.01
clip_norm = 0.5

F32 = jnp.float32
BF16 = jnp.bfloat16


def window(tile):
    lane = tile * 128
    source = OWN * (lane // PAD) + min(lane % PAD, OWN - 1)
    low = source // 128 * 128
    return low, min(256, D - low)


def spread_matrix():
    out = np.zeros((TILES, 128, 256), np.float32)
    for tile in range(TILES):
        low, width = window(tile)
        for lane in range(128):
            chunk, row = divmod(tile * 128 + lane, PAD)
            if row < OWN:
                at = chunk * OWN + row - low
                assert 0 <= at < width
                out[tile, lane, at] = 1
    return out


def ring_plan(n):
    plan = []
    for way in (1, -1):
        for half in (0, 1):
            far = n // 2 if (way == 1) == (half == 0) else n // 2 - 1
            plan.append((way, half, far))
    return plan


class Ring:
    def __init__(self, n, at, view, landing, send_sem, recv_sem, first_sem, to):
        self.n, self.at, self.view, self.landing = n, at, view, landing
        self.send_sem, self.recv_sem, self.to = send_sem, recv_sem, to
        self.slots = {}
        slot = 0
        for way, half, far in ring_plan(n):
            for step in range(far):
                self.slots[way, half, step] = (slot, first_sem + slot)
                slot += 1
        self.copies = {}

    def step(self, count):
        for longest in (True, False):
            for way, half, far in ring_plan(self.n):
                step = count
                if (far == self.n // 2) != longest or step > far:
                    continue
                left = far - step
                target = lax.rem(self.at + way * left + self.n, self.n)
                mine = self.view(target, half)
                if step > 0:
                    self.copies[way, half, step - 1].wait_recv()
                    slot, _ = self.slots[way, half, step - 1]
                    mine[...] = mine[...] + self.landing.at[slot][...]
                if left > 0:
                    slot, sem = self.slots[way, half, step]
                    copy = pltpu.make_async_remote_copy(
                        src_ref=mine,
                        dst_ref=self.landing.at[slot],
                        send_sem=self.send_sem.at[sem],
                        recv_sem=self.recv_sem.at[sem],
                        device_id=self.to(way),
                        device_id_type=pl.DeviceIdType.MESH,
                    )
                    copy.start()
                    self.copies[way, half, step] = copy

    def finish(self):
        for copy in self.copies.values():
            copy.wait_send()


def kernel(
    acts, queries, keys, out_grad, positions, bands, step, weight, one, two, spread,
    out, mean_weight, mean_one, mean_two,
    acts_pad, acts_t, k2, v2, probs, dist, dv, dv_send, dv_recv, dv_half, key_halo, value_send, value_halo,
    whole, ga, gb, ra, rb, ra2, rb2, moments, grads, n_send, n_one, n_two_send, n_two, norms,
    send_sem, recv_sem,
):
    ctx = lax.axis_index("ctx")
    wrk = lax.axis_index("work")
    z, y, x = ctx // (NY * NX), lax.rem(ctx // NX, NY), lax.rem(ctx, NX)
    zh, core = wrk // 2, lax.rem(wrk, 2)
    zx, zy = z * NX + x, z * NY + y
    nxt = lax.rem(ctx + 1, NCTX)
    prv = lax.rem(ctx + NCTX - 1, NCTX)

    def at_ctx(zz, yy, xx):
        return {"ctx": (zz * NY + yy) * NX + xx}

    def zx_peer(k):
        other = lax.rem(zx + k, NZ * NX)
        return other // NX, lax.rem(other, NX)

    def zy_peer(k):
        other = lax.rem(zy + k, NZ * NY)
        return other // NY, lax.rem(other, NY)

    used = [0]
    pending = []

    def send(src, dst, device):
        sem = used[0]
        used[0] += 1
        copy = pltpu.make_async_remote_copy(
            src_ref=src,
            dst_ref=dst,
            send_sem=send_sem.at[sem],
            recv_sem=recv_sem.at[sem],
            device_id=device,
            device_id_type=pl.DeviceIdType.MESH,
        )
        copy.start()
        pending.append(copy)
        return copy

    barrier = pltpu.get_barrier_semaphore()
    greeted = [{"ctx": nxt}, {"ctx": prv}]
    for k in range(1, NZ * NX):
        zz, xx = zx_peer(k)
        greeted.append(at_ctx(zz, y, xx))
    for k in range(1, NZ * NY):
        zz, yy = zy_peer(k)
        greeted.append(at_ctx(zz, yy, x))
    for k in range(1, NW):
        greeted.append({"work": lax.rem(wrk + k, NW)})
    for device in greeted:
        pl.semaphore_signal(barrier, inc=1, device_id=device, device_id_type=pl.DeviceIdType.MESH)

    low_lane = lax.broadcasted_iota(jnp.int32, (1, 128), 1) < HD

    def widen(source, target, first, count):
        for pair in range(KH // 2):
            tile = source[:, pair * 128 : pair * 128 + 128].astype(F32)
            other = pltpu.roll(tile, HD, 1)
            at = pl.ds(first, count)
            target[2 * pair, 0, at, :] = jnp.where(low_lane, tile, 0.0).astype(BF16)
            target[2 * pair, 1, at, :] = jnp.where(low_lane, 0.0, other).astype(BF16)
            target[2 * pair + 1, 0, at, :] = jnp.where(low_lane, other, 0.0).astype(BF16)
            target[2 * pair + 1, 1, at, :] = jnp.where(low_lane, 0.0, tile).astype(BF16)

    spare = jnp.zeros((PAD - OWN, KH * HD), F32)
    for index, source in enumerate((weight, one, two)):
        moments[zh, core, index] = jnp.concatenate([source[...], spare], 0)
    whole[z, y, x] = jnp.concatenate([weight[...], spare], 0).astype(BF16)
    widen(keys[...], k2, SPAN, ROWS)
    for block in range(2):
        apart = (
            lax.broadcasted_iota(jnp.int32, (ROWS, SPAN), 1)
            + SPAN
            - lax.broadcasted_iota(jnp.int32, (ROWS, SPAN), 0)
        )
        near = (apart >= 0) & (apart <= positions[:, block * SPAN : block * SPAN + SPAN])
        dist[block] = jnp.where(near, apart, 1 << 20)

    pl.semaphore_wait(barrier, len(greeted))

    keys_in = send(keys.at[pl.ds(ROWS - SPAN, SPAN)], key_halo, {"ctx": nxt})
    whole_y = [
        send(whole.at[z, y, x], whole.at[z, y, x], at_ctx(z, lax.rem(y + k, NY), x)) for k in range(1, NY)
    ]

    def over_work(buffer):
        far = [
            send(buffer.at[zh, core], buffer.at[zh, core], {"work": lax.rem(zh + k, NH) * 2 + core})
            for k in range(1, NH)
        ]
        near = [send(buffer.at[zh, core], buffer.at[zh, core], {"work": zh * 2 + 1 - core})]

        def forward():
            for k in range(1, NH):
                far[k - 1].wait_recv()
                source = lax.rem(zh + NH - k, NH)
                near.append(
                    send(buffer.at[source, core], buffer.at[source, core], {"work": zh * 2 + 1 - core})
                )

        def arrive():
            for copy in near:
                copy.wait_recv()

        return forward, arrive

    moments_forward, moments_arrive = over_work(moments)

    for tile in range(TILES):
        low, width = window(tile)
        acts_t[tile * 128 : tile * 128 + 128, :] = lax.dot_general(
            spread[tile, :, :width],
            acts[:, low : low + width],
            (((1,), (1,)), ((), ())),
            preferred_element_type=F32,
        ).astype(BF16)

    factor = HD**-0.5 * math.log2(math.e)

    def attend(pair, block):
        rows = slice(block * SPAN, block * SPAN + SPAN)
        span = slice(block * SPAN, block * SPAN + ROWS)

        def head(index, carry):
            j = 2 * pair + index
            first = pl.multiple_of(j * 512, 512)
            for i in range(4):
                query = queries[rows, pl.ds(pl.multiple_of(first + i * 128, 128), 128)]
                for e in range(2):
                    scores = lax.dot_general(
                        k2[j, e, span, :], query, (((1,), (1,)), ((), ())), preferred_element_type=F32
                    )
                    scores = jnp.where(dist[block] <= bands[j * 8 + 2 * i + e], scores, -1e30)
                    top = jnp.max(scores, axis=0, keepdims=True)
                    expo = jnp.exp2((scores - top) * factor)
                    total = jnp.sum(expo, axis=0, keepdims=True)
                    probs[block, j, e, :, i * 128 : i * 128 + 128] = (expo * (1.0 / total)).astype(BF16)
            cotan = jnp.concatenate(
                [out_grad[rows, pl.ds(pl.multiple_of(first + i * 128, 128), 128)] for i in range(4)], 0
            )
            even = jnp.dot(probs[block, j, 0], cotan, preferred_element_type=F32)
            odd = jnp.dot(probs[block, j, 1], cotan, preferred_element_type=F32)
            dv[block, j] = even + pltpu.roll(odd, HD, 1)
            return carry

        lax.fori_loop(0, 2, head, 0)

    def joined(pair, block):
        return jnp.where(low_lane, dv[block, 2 * pair], pltpu.roll(dv[block, 2 * pair + 1], HD, 1))

    def halo_back(pair):
        dv_send[pair] = joined(pair, 0)[:SPAN]
        return send(dv_send.at[pair], dv_recv.at[pair], {"ctx": prv})

    def value_grad(pair, halo):
        first, second = joined(pair, 0), joined(pair, 1)
        halo.wait_recv()
        dv_half[pair, :SPAN, :] = (first[SPAN:] + second[:SPAN]).astype(BF16)
        dv_half[pair, SPAN:, :] = (second[SPAN:] + dv_recv[pair]).astype(BF16)

    attend(0, 1)
    keys_in.wait_recv()
    widen(key_halo[...], k2, 0, SPAN)
    attend(0, 0)
    halo_a = halo_back(0)
    for copy in whole_y:
        copy.wait_recv()
    whole_x = [
        send(whole.at[z, :, x], whole.at[z, :, x], at_ctx(z, y, lax.rem(x + k, NX))) for k in range(1, NX)
    ]
    attend(1, 1)
    value_grad(0, halo_a)

    def grad_a(i, carry):
        rows = pl.ds(pl.multiple_of(i * 768, 768), 768)
        ga[pl.ds(i * 4, 4)] = jnp.dot(acts_t[rows, :], dv_half[0], preferred_element_type=F32).reshape(
            4, NX, PAD, 128
        )
        return carry

    lax.fori_loop(0, 4, grad_a, 0)
    ring_a = Ring(
        NY, y, lambda t, h: ga.at[h * NY + t], ra, send_sem, recv_sem, 100,
        lambda way: at_ctx(z, lax.rem(y + way + NY, NY), x),
    )
    ring_a.step(0)
    attend(1, 0)
    halo_b = halo_back(1)
    moments_forward()
    ring_a.step(1)
    for copy in whole_x:
        copy.wait_recv()
    whole_z = send(whole.at[z], whole.at[z], at_ctx(1 - z, y, x))
    value_grad(1, halo_b)

    def grad_b(i, carry):
        for h in range(NZ):
            rows = pl.ds(pl.multiple_of(h * 1536 + i * 384, 384), 384)
            block = jnp.dot(acts_t[rows, :], dv_half[1], preferred_element_type=F32).reshape(
                2, NX, PAD, 128
            )
            for t in range(NX):
                gb[h, t, pl.ds(i * 2, 2)] = block[:, t]
        return carry

    lax.fori_loop(0, 4, grad_b, 0)
    ring_b = Ring(
        NX, x, lambda t, h: gb.at[h, t], rb, send_sem, recv_sem, 114,
        lambda way: at_ctx(z, y, lax.rem(x + way + NX, NX)),
    )
    ring_b.step(0)
    ring_a.step(2)
    ring_b.step(1)
    for tile in range(TILES):
        low, width = window(tile)
        acts_pad[:, tile * 128 : tile * 128 + 128] = lax.dot_general(
            acts[:, low : low + width],
            spread[tile, :, :width],
            (((1,), (1,)), ((), ())),
            preferred_element_type=F32,
        ).astype(BF16)
    ring_a.step(3)
    ring_b.step(2)
    ring_a.step(4)

    second_a = []
    for k in range(1, NZ * NX):
        zz, xx = zx_peer(k)
        second_a.append(send(ga.at[zz * NY + y, xx], ra2.at[k - 1], at_ctx(zz, y, xx)))
    second_b = []
    for k in range(1, NZ * NY):
        zz, yy = zy_peer(k)
        second_b.append(send(gb.at[zz, x, yy], rb2.at[k - 1], at_ctx(zz, yy, x)))

    whole_z.wait_recv()
    values = jnp.dot(
        acts_pad[...], whole[...].reshape(NCTX * PAD, KH * HD), preferred_element_type=F32
    ).astype(BF16)
    value_send[...] = values[ROWS - SPAN :]
    values_in = send(value_send, value_halo, {"ctx": nxt})
    widen(values, v2, SPAN, ROWS)

    def output(block):
        rows = slice(block * SPAN, block * SPAN + SPAN)
        span = slice(block * SPAN, block * SPAN + ROWS)

        def head(j, carry):
            total = jnp.zeros((512, 128), F32)
            for e in range(2):
                total += lax.dot_general(
                    probs[block, j, e], v2[j, e, span, :], (((0,), (0,)), ((), ())), preferred_element_type=F32
                )
            for i in range(4):
                out[rows, pl.ds(pl.multiple_of(j * 512 + i * 128, 128), 128)] = total[
                    i * 128 : i * 128 + 128
                ].astype(BF16)
            return carry

        lax.fori_loop(0, KH, head, 0)

    output(1)
    for copy in second_a:
        copy.wait_recv()
    half_a = ga[z * NY + y, x]
    for k in range(1, NZ * NX):
        half_a = half_a + ra2[k - 1]
    for copy in second_b:
        copy.wait_recv()
    half_b = gb[z, x, y]
    for k in range(1, NZ * NY):
        half_b = half_b + rb2[k - 1]
    tokens_all = float(ROWS * NCTX)
    half_a, half_b = half_a / tokens_all, half_b / tokens_all
    grads[zh, core, :, :128] = half_a
    grads[zh, core, :, 128:] = half_b
    grads_forward, grads_arrive = over_work(grads)
    n_send[...] = (half_a * half_a + half_b * half_b).reshape(PAD // 8, 8, 128).sum(0)
    norm_one = []
    for k in range(1, NZ * NX):
        zz, xx = zx_peer(k)
        norm_one.append(send(n_send, n_one.at[k - 1], at_ctx(zz, y, xx)))
    values_in.wait_recv()
    widen(value_halo[...], v2, 0, SPAN)
    for copy in norm_one:
        copy.wait_recv()
    n_two_send[...] = n_send[...] + n_one[...].sum(0)
    norm_two = [
        send(n_two_send, n_two.at[k - 1], at_ctx(z, lax.rem(y + k, NY), x)) for k in range(1, NY)
    ]
    grads_forward()
    for copy in norm_two:
        copy.wait_recv()
    norms[wrk] = n_two_send[...] + n_two[...].sum(0)
    norm_work = [
        send(norms.at[wrk], norms.at[wrk], {"work": lax.rem(wrk + k, NW)}) for k in range(1, NW)
    ]
    output(0)
    moments_arrive()
    grads_arrive()
    for copy in norm_work:
        copy.wait_recv()

    count = jnp.full((1, 128), step[0].astype(F32), F32)
    fix_one = (1.0 - jnp.exp(count * math.log(beta_one)))[:, :1]
    fix_two = (1.0 - jnp.exp(count * math.log(beta_two)))[:, :1]
    sums = [jnp.zeros((PAD, KH * HD), F32) for _ in range(3)]
    for w in range(NW):
        square = jnp.sum(jnp.sum(norms[w], axis=0, keepdims=True), axis=1, keepdims=True)
        scale = jnp.minimum(1.0, clip_norm / (jnp.sqrt(square) + 1e-06))
        grad = grads[w // 2, w % 2] * scale
        first = beta_one * moments[w // 2, w % 2, 1] + (1.0 - beta_one) * grad
        second = beta_two * moments[w // 2, w % 2, 2] + (1.0 - beta_two) * grad * grad
        updated = moments[w // 2, w % 2, 0] - learn_rate * (first / fix_one) / (
            jnp.sqrt(second / fix_two) + adam_eps
        )
        sums = [total + part for total, part in zip(sums, (updated, first, second))]
    for target, total in zip((mean_weight, mean_one, mean_two), sums):
        target[...] = (total / NW)[:OWN]

    for copy in pending:
        copy.wait_send()
    ring_a.finish()
    ring_b.finish()


def per_device(
    inputs, queries, keys, out_grad, positions, bands, step, value_weight, moment_one, moment_two
):
    vmem = pl.BlockSpec(memory_space=pltpu.VMEM)
    smem = pl.BlockSpec(memory_space=pltpu.SMEM)
    width = KH * HD
    out, mean_weight, mean_one, mean_two = pl.pallas_call(
        kernel,
        out_shape=(
            jax.ShapeDtypeStruct((ROWS, QH * HD), BF16),
            *[jax.ShapeDtypeStruct((OWN, width), F32)] * 3,
        ),
        in_specs=[vmem, vmem, vmem, vmem, vmem, smem, smem, vmem, vmem, vmem, vmem],
        out_specs=(vmem, vmem, vmem, vmem),
        scratch_shapes=[
            pltpu.VMEM((ROWS, NCTX * PAD), BF16),
            pltpu.VMEM((NCTX * PAD, ROWS), BF16),
            pltpu.VMEM((KH, 2, SPAN + ROWS, 128), BF16),
            pltpu.VMEM((KH, 2, SPAN + ROWS, 128), BF16),
            pltpu.VMEM((2, KH, 2, ROWS, 512), BF16),
            pltpu.VMEM((2, ROWS, SPAN), jnp.int32),
            pltpu.VMEM((2, KH, ROWS, 128), F32),
            pltpu.VMEM((2, SPAN, 128), F32),
            pltpu.VMEM((2, SPAN, 128), F32),
            pltpu.VMEM((2, ROWS, 128), BF16),
            pltpu.VMEM((SPAN, width), BF16),
            pltpu.VMEM((SPAN, width), BF16),
            pltpu.VMEM((SPAN, width), BF16),
            pltpu.VMEM((NZ, NY, NX, PAD, width), BF16),
            pltpu.VMEM((NZ * NY, NX, PAD, 128), F32),
            pltpu.VMEM((NZ, NX, NY, PAD, 128), F32),
            pltpu.VMEM((14, NX, PAD, 128), F32),
            pltpu.VMEM((6, NY, PAD, 128), F32),
            pltpu.VMEM((NZ * NX - 1, PAD, 128), F32),
            pltpu.VMEM((NZ * NY - 1, PAD, 128), F32),
            pltpu.VMEM((NH, 2, 3, PAD, width), F32),
            pltpu.VMEM((NH, 2, PAD, width), F32),
            pltpu.VMEM((8, 128), F32),
            pltpu.VMEM((NZ * NX - 1, 8, 128), F32),
            pltpu.VMEM((8, 128), F32),
            pltpu.VMEM((NY - 1, 8, 128), F32),
            pltpu.VMEM((NW, 8, 128), F32),
            pltpu.SemaphoreType.DMA((120,)),
            pltpu.SemaphoreType.DMA((120,)),
        ],
        compiler_params=pltpu.CompilerParams(
            collective_id=0, has_side_effects=True, vmem_limit_bytes=48 * 1024 * 1024
        ),
        name="local_adam",
    )(
        inputs[0], queries[0], keys[0], out_grad[0], positions, bands, step,
        value_weight[0], moment_one[0], moment_two[0], jnp.asarray(spread_matrix(), BF16),
    )
    return out[None], mean_weight, mean_one, mean_two


def solution(mesh):
    rows = P("work", "ctx", None)
    in_specs = (rows, rows, rows, rows, P("work", "ctx"), P(), P(), rows, rows, rows)
    out_specs = (rows, P("ctx", None), P("ctx", None), P("ctx", None))
    return jax.shard_map(
        per_device, mesh=mesh, in_specs=in_specs, out_specs=out_specs, check_vma=False
    )
```

```python
import functools
import math

import jax
import jax.numpy as jnp
import numpy as np
from jax import lax
from jax.experimental import pallas as pl
from jax.experimental.pallas import tpu as pltpu
from jax.sharding import PartitionSpec as P

D = 2880
HD = 64
QH = 32
KH = 4
SPAN = 128
ROWS = 256
NZ, NY, NX = 2, 8, 4
NCTX = NZ * NY * NX
NH = 4
NW = 8
OWN = D // NCTX
PAD = 48
TILES = NCTX * PAD // 128

beta_one = 0.9
beta_two = 0.95
adam_eps = 1e-08
learn_rate = 0.01
clip_norm = 0.5

F32 = jnp.float32
BF16 = jnp.bfloat16


def window(tile):
    lane = tile * 128
    source = OWN * (lane // PAD) + min(lane % PAD, OWN - 1)
    low = source // 128 * 128
    return low, min(256, D - low)


def spread_matrix():
    out = np.zeros((TILES, 128, 256), np.float32)
    for tile in range(TILES):
        low, width = window(tile)
        for lane in range(128):
            chunk, row = divmod(tile * 128 + lane, PAD)
            if row < OWN:
                at = chunk * OWN + row - low
                assert 0 <= at < width
                out[tile, lane, at] = 1
    return out


def ring_plan(n):
    plan = []
    for way in (1, -1):
        for half in (0, 1):
            far = n // 2 if (way == 1) == (half == 0) else n // 2 - 1
            plan.append((way, half, far))
    return plan


class Ring:
    def __init__(self, n, at, view, landing, send_sem, recv_sem, first_sem, to):
        self.n, self.at, self.view, self.landing = n, at, view, landing
        self.send_sem, self.recv_sem, self.to = send_sem, recv_sem, to
        self.slots = {}
        slot = 0
        for way, half, far in ring_plan(n):
            for step in range(far):
                self.slots[way, half, step] = (slot, first_sem + slot)
                slot += 1
        self.copies = {}

    def step(self, count):
        for longest in (True, False):
            for way, half, far in ring_plan(self.n):
                step = count
                if (far == self.n // 2) != longest or step > far:
                    continue
                left = far - step
                target = lax.rem(self.at + way * left + self.n, self.n)
                mine = self.view(target, half)
                if step > 0:
                    self.copies[way, half, step - 1].wait_recv()
                    slot, _ = self.slots[way, half, step - 1]
                    mine[...] = mine[...] + self.landing.at[slot][...]
                if left > 0:
                    slot, sem = self.slots[way, half, step]
                    copy = pltpu.make_async_remote_copy(
                        src_ref=mine,
                        dst_ref=self.landing.at[slot],
                        send_sem=self.send_sem.at[sem],
                        recv_sem=self.recv_sem.at[sem],
                        device_id=self.to(way),
                        device_id_type=pl.DeviceIdType.MESH,
                    )
                    copy.start()
                    self.copies[way, half, step] = copy

    def finish(self):
        for copy in self.copies.values():
            copy.wait_send()


def kernel(
    acts_hbm, queries_hbm, keys_hbm, out_grad_hbm, positions_hbm, bands, step, weight_hbm, one_hbm, two_hbm, spread_hbm,
    out_hbm, mean_weight, mean_one, mean_two,
    out, acts, queries, keys, out_grad, positions, state, spread, acts_t, k2, v2, probs, dist, dv, dv_send, dv_recv, dv_half, key_halo, value_send, value_halo,
    whole, ga, gb, ra, rb, ra2, rb2, moments, grads, n_send, n_one, n_two_send, n_two, norms,
    send_sem, recv_sem, load_sem,
):
    ctx = lax.axis_index("ctx")
    wrk = lax.axis_index("work")
    z, y, x = ctx // (NY * NX), lax.rem(ctx // NX, NY), lax.rem(ctx, NX)
    zh, core = wrk // 2, lax.rem(wrk, 2)
    zx, zy = z * NX + x, z * NY + y
    nxt = lax.rem(ctx + 1, NCTX)
    prv = lax.rem(ctx + NCTX - 1, NCTX)

    def at_ctx(zz, yy, xx):
        return {"ctx": (zz * NY + yy) * NX + xx}

    def zx_peer(k):
        other = lax.rem(zx + k, NZ * NX)
        return other // NX, lax.rem(other, NX)

    def zy_peer(k):
        other = lax.rem(zy + k, NZ * NY)
        return other // NY, lax.rem(other, NY)

    used = [0]
    pending = []

    def send(src, dst, device):
        sem = used[0]
        used[0] += 1
        copy = pltpu.make_async_remote_copy(
            src_ref=src,
            dst_ref=dst,
            send_sem=send_sem.at[sem],
            recv_sem=recv_sem.at[sem],
            device_id=device,
            device_id_type=pl.DeviceIdType.MESH,
        )
        copy.start()
        pending.append(copy)
        return copy

    loads = []
    for index, (source, target) in enumerate((
        (keys_hbm, keys), (positions_hbm, positions), (queries_hbm, queries), (out_grad_hbm, out_grad),
        (weight_hbm, state.at[0]), (one_hbm, state.at[1]), (two_hbm, state.at[2]),
        (spread_hbm, spread), (acts_hbm, acts),
    )):
        load = pltpu.make_async_copy(source, target, load_sem.at[index])
        load.start()
        loads.append(load)

    barrier = pltpu.get_barrier_semaphore()
    greeted = [{"ctx": nxt}, {"ctx": prv}]
    for k in range(1, NZ * NX):
        zz, xx = zx_peer(k)
        greeted.append(at_ctx(zz, y, xx))
    for k in range(1, NZ * NY):
        zz, yy = zy_peer(k)
        greeted.append(at_ctx(zz, yy, x))
    for k in range(1, NW):
        greeted.append({"work": lax.rem(wrk + k, NW)})
    for device in greeted:
        pl.semaphore_signal(barrier, inc=1, device_id=device, device_id_type=pl.DeviceIdType.MESH)

    low_lane = lax.broadcasted_iota(jnp.int32, (1, 128), 1) < HD

    def widen(source, target, first, count):
        for pair in range(KH // 2):
            tile = source[:, pair * 128 : pair * 128 + 128].astype(F32)
            other = pltpu.roll(tile, HD, 1)
            at = pl.ds(first, count)
            target[2 * pair, 0, at, :] = jnp.where(low_lane, tile, 0.0).astype(BF16)
            target[2 * pair, 1, at, :] = jnp.where(low_lane, 0.0, other).astype(BF16)
            target[2 * pair + 1, 0, at, :] = jnp.where(low_lane, other, 0.0).astype(BF16)
            target[2 * pair + 1, 1, at, :] = jnp.where(low_lane, 0.0, tile).astype(BF16)

    for load in loads[:2]:
        load.wait()
    widen(keys[...], k2, SPAN, ROWS)
    for block in range(2):
        apart = (
            lax.broadcasted_iota(jnp.int32, (ROWS, SPAN), 1)
            + SPAN
            - lax.broadcasted_iota(jnp.int32, (ROWS, SPAN), 0)
        )
        near = (apart >= 0) & (apart <= positions[:, block * SPAN : block * SPAN + SPAN])
        dist[block] = jnp.where(near, apart, 1 << 20)

    factor = HD**-0.5 * math.log2(math.e)

    def attend(pair, block):
        rows = slice(block * SPAN, block * SPAN + SPAN)
        span = slice(block * SPAN, block * SPAN + ROWS)

        def head(index, carry):
            j = 2 * pair + index
            first = pl.multiple_of(j * 512, 512)
            for i in range(4):
                query = queries[rows, pl.ds(pl.multiple_of(first + i * 128, 128), 128)]
                for e in range(2):
                    scores = lax.dot_general(
                        k2[j, e, span, :], query, (((1,), (1,)), ((), ())), preferred_element_type=F32
                    )
                    scores = jnp.where(dist[block] <= bands[j * 8 + 2 * i + e], scores, -1e30)
                    top = jnp.max(scores, axis=0, keepdims=True)
                    expo = jnp.exp2((scores - top) * factor)
                    total = jnp.sum(expo, axis=0, keepdims=True)
                    probs[block, j, e, :, i * 128 : i * 128 + 128] = (expo * (1.0 / total)).astype(BF16)
            cotan = jnp.concatenate(
                [out_grad[rows, pl.ds(pl.multiple_of(first + i * 128, 128), 128)] for i in range(4)], 0
            )
            even = jnp.dot(probs[block, j, 0], cotan, preferred_element_type=F32)
            odd = jnp.dot(probs[block, j, 1], cotan, preferred_element_type=F32)
            dv[block, j] = even + pltpu.roll(odd, HD, 1)
            return carry

        lax.fori_loop(0, 2, head, 0)

    def joined(pair, block):
        return jnp.where(low_lane, dv[block, 2 * pair], pltpu.roll(dv[block, 2 * pair + 1], HD, 1))

    def halo_back(pair):
        dv_send[pair] = joined(pair, 0)[:SPAN]
        return send(dv_send.at[pair], dv_recv.at[pair], {"ctx": prv})

    def value_grad(pair, halo):
        first, second = joined(pair, 0), joined(pair, 1)
        halo.wait_recv()
        dv_half[pair, :SPAN, :] = (first[SPAN:] + second[:SPAN]).astype(BF16)
        dv_half[pair, SPAN:, :] = (second[SPAN:] + dv_recv[pair]).astype(BF16)

    for load in loads[2:4]:
        load.wait()
    attend(0, 1)
    for load in loads[4:7]:
        load.wait()
    spare = jnp.zeros((PAD - OWN, KH * HD), F32)
    for index in range(3):
        moments[zh, core, index] = jnp.concatenate([state[index, :, 0, :], spare], 0)
    whole[z, y, x] = moments[zh, core, 0].astype(BF16)

    pl.semaphore_wait(barrier, len(greeted))

    keys_in = send(keys.at[pl.ds(ROWS - SPAN, SPAN)], key_halo, {"ctx": nxt})
    whole_y = [
        send(whole.at[z, y, x], whole.at[z, y, x], at_ctx(z, lax.rem(y + k, NY), x)) for k in range(1, NY)
    ]

    def over_work(buffer):
        far = [
            send(buffer.at[zh, core], buffer.at[zh, core], {"work": lax.rem(zh + k, NH) * 2 + core})
            for k in range(1, NH)
        ]
        near = [send(buffer.at[zh, core], buffer.at[zh, core], {"work": zh * 2 + 1 - core})]

        def forward():
            for k in range(1, NH):
                far[k - 1].wait_recv()
                source = lax.rem(zh + NH - k, NH)
                near.append(
                    send(buffer.at[source, core], buffer.at[source, core], {"work": zh * 2 + 1 - core})
                )

        def arrive():
            for copy in near:
                copy.wait_recv()

        return forward, arrive

    moments_forward, moments_arrive = over_work(moments)

    for load in loads[7:]:
        load.wait()
    for tile in range(TILES):
        low, width = window(tile)
        acts_t[tile * 128 : tile * 128 + 128, :] = jnp.dot(
            spread[tile, :, :width], acts[low : low + width, :], preferred_element_type=F32
        ).astype(BF16)
    attend(1, 1)
    keys_in.wait_recv()
    widen(key_halo[...], k2, 0, SPAN)
    attend(0, 0)
    halo_a = halo_back(0)
    attend(1, 0)
    halo_b = halo_back(1)
    for copy in whole_y:
        copy.wait_recv()
    whole_x = [
        send(whole.at[z, :, x], whole.at[z, :, x], at_ctx(z, y, lax.rem(x + k, NX))) for k in range(1, NX)
    ]
    value_grad(0, halo_a)

    def grad_a(i, carry):
        rows = pl.ds(pl.multiple_of(i * 768, 768), 768)
        ga[pl.ds(i * 4, 4)] = jnp.dot(acts_t[rows, :], dv_half[0], preferred_element_type=F32).reshape(
            4, NX, PAD, 128
        )
        return carry

    lax.fori_loop(0, 4, grad_a, 0)
    ring_a = Ring(
        NY, y, lambda t, h: ga.at[h * NY + t], ra, send_sem, recv_sem, 100,
        lambda way: at_ctx(z, lax.rem(y + way + NY, NY), x),
    )
    ring_a.step(0)
    value_grad(1, halo_b)

    def grad_b(i, carry):
        for h in range(NZ):
            rows = pl.ds(pl.multiple_of(h * 1536 + i * 384, 384), 384)
            block = jnp.dot(acts_t[rows, :], dv_half[1], preferred_element_type=F32).reshape(
                2, NX, PAD, 128
            )
            for t in range(NX):
                gb[h, t, pl.ds(i * 2, 2)] = block[:, t]
        return carry

    lax.fori_loop(0, 4, grad_b, 0)
    ring_b = Ring(
        NX, x, lambda t, h: gb.at[h, t], rb, send_sem, recv_sem, 114,
        lambda way: at_ctx(z, y, lax.rem(x + way + NX, NX)),
    )
    ring_b.step(0)
    moments_forward()
    ring_a.step(1)
    for copy in whole_x:
        copy.wait_recv()
    whole_z = send(whole.at[z], whole.at[z], at_ctx(1 - z, y, x))
    ring_a.step(2)
    ring_b.step(1)
    ring_a.step(3)
    ring_b.step(2)
    ring_a.step(4)

    second_a = []
    for k in range(1, NZ * NX):
        zz, xx = zx_peer(k)
        second_a.append(send(ga.at[zz * NY + y, xx], ra2.at[k - 1], at_ctx(zz, y, xx)))
    second_b = []
    for k in range(1, NZ * NY):
        zz, yy = zy_peer(k)
        second_b.append(send(gb.at[zz, x, yy], rb2.at[k - 1], at_ctx(zz, yy, x)))

    whole_z.wait_recv()
    values = lax.dot_general(
        acts_t[...], whole[...].reshape(NCTX * PAD, KH * HD), (((0,), (0,)), ((), ())), preferred_element_type=F32
    ).astype(BF16)
    value_send[...] = values[ROWS - SPAN :]
    values_in = send(value_send, value_halo, {"ctx": nxt})
    widen(values, v2, SPAN, ROWS)

    def output(block):
        rows = slice(block * SPAN, block * SPAN + SPAN)
        span = slice(block * SPAN, block * SPAN + ROWS)

        def head(j, carry):
            total = jnp.zeros((512, 128), F32)
            for e in range(2):
                total += lax.dot_general(
                    probs[block, j, e], v2[j, e, span, :], (((0,), (0,)), ((), ())), preferred_element_type=F32
                )
            for i in range(4):
                out[rows, pl.ds(pl.multiple_of(j * 512 + i * 128, 128), 128)] = total[
                    i * 128 : i * 128 + 128
                ].astype(BF16)
            return carry

        lax.fori_loop(0, KH, head, 0)

    for copy in second_a:
        copy.wait_recv()
    half_a = ga[z * NY + y, x]
    for k in range(1, NZ * NX):
        half_a = half_a + ra2[k - 1]
    for copy in second_b:
        copy.wait_recv()
    half_b = gb[z, x, y]
    for k in range(1, NZ * NY):
        half_b = half_b + rb2[k - 1]
    tokens_all = float(ROWS * NCTX)
    half_a, half_b = half_a / tokens_all, half_b / tokens_all
    grads[zh, core, :, :128] = half_a
    grads[zh, core, :, 128:] = half_b
    grads_forward, grads_arrive = over_work(grads)
    n_send[...] = (half_a * half_a + half_b * half_b).reshape(PAD // 8, 8, 128).sum(0)
    norm_one = []
    for k in range(1, NZ * NX):
        zz, xx = zx_peer(k)
        norm_one.append(send(n_send, n_one.at[k - 1], at_ctx(zz, y, xx)))
    output(1)
    values_in.wait_recv()
    widen(value_halo[...], v2, 0, SPAN)
    for copy in norm_one:
        copy.wait_recv()
    n_two_send[...] = n_send[...] + n_one[...].sum(0)
    norm_two = [
        send(n_two_send, n_two.at[k - 1], at_ctx(z, lax.rem(y + k, NY), x)) for k in range(1, NY)
    ]
    grads_forward()
    output(0)
    store = pltpu.make_async_copy(out, out_hbm, load_sem.at[9])
    store.start()
    for copy in norm_two:
        copy.wait_recv()
    norms[wrk] = n_two_send[...] + n_two[...].sum(0)
    norm_work = [
        send(norms.at[wrk], norms.at[wrk], {"work": lax.rem(wrk + k, NW)}) for k in range(1, NW)
    ]
    moments_arrive()
    grads_arrive()
    for copy in norm_work:
        copy.wait_recv()

    count = jnp.full((1, 128), step[0].astype(F32), F32)
    fix_one = (1.0 - jnp.exp(count * math.log(beta_one)))[:, :1]
    fix_two = (1.0 - jnp.exp(count * math.log(beta_two)))[:, :1]
    sums = [jnp.zeros((PAD, KH * HD), F32) for _ in range(3)]
    for w in range(NW):
        square = jnp.sum(jnp.sum(norms[w], axis=0, keepdims=True), axis=1, keepdims=True)
        scale = jnp.minimum(1.0, clip_norm / (jnp.sqrt(square) + 1e-06))
        grad = grads[w // 2, w % 2] * scale
        first = beta_one * moments[w // 2, w % 2, 1] + (1.0 - beta_one) * grad
        second = beta_two * moments[w // 2, w % 2, 2] + (1.0 - beta_two) * grad * grad
        updated = moments[w // 2, w % 2, 0] - learn_rate * (first / fix_one) / (
            jnp.sqrt(second / fix_two) + adam_eps
        )
        sums = [total + part for total, part in zip(sums, (updated, first, second))]
    for target, total in zip((mean_weight, mean_one, mean_two), sums):
        target[...] = (total / NW)[:OWN]

    store.wait()
    for copy in pending:
        copy.wait_send()
    ring_a.finish()
    ring_b.finish()


def hand_over(*refs):
    sems = refs[-1]
    copies = [pltpu.make_async_copy(refs[i], refs[4 + i], sems.at[i]) for i in range(4)]
    for copy in copies:
        copy.start()
    for copy in copies:
        copy.wait()


def per_device(
    inputs, queries, keys, out_grad, positions, bands, step, value_weight, moment_one, moment_two
):
    vmem = pl.BlockSpec(memory_space=pltpu.VMEM)
    hbm = pl.BlockSpec(memory_space=pltpu.HBM)
    smem = pl.BlockSpec(memory_space=pltpu.SMEM)
    width = KH * HD
    out, mean_weight, mean_one, mean_two = pl.pallas_call(
        kernel,
        out_shape=(
            jax.ShapeDtypeStruct((ROWS, QH * HD), BF16),
            *[jax.ShapeDtypeStruct((OWN, width), F32)] * 3,
        ),
        in_specs=[hbm, hbm, hbm, hbm, hbm, smem, smem, hbm, hbm, hbm, hbm],
        out_specs=(hbm, vmem, vmem, vmem),
        scratch_shapes=[
            pltpu.VMEM((ROWS, QH * HD), BF16),
            pltpu.VMEM((D, ROWS), BF16),
            pltpu.VMEM((ROWS, QH * HD), BF16),
            pltpu.VMEM((ROWS, width), BF16),
            pltpu.VMEM((ROWS, QH * HD), BF16),
            pltpu.VMEM((1, ROWS), jnp.int32),
            pltpu.VMEM((3, OWN, 1, width), F32),
            pltpu.VMEM((TILES, 128, 256), BF16),
            pltpu.VMEM((NCTX * PAD, ROWS), BF16),
            pltpu.VMEM((KH, 2, SPAN + ROWS, 128), BF16),
            pltpu.VMEM((KH, 2, SPAN + ROWS, 128), BF16),
            pltpu.VMEM((2, KH, 2, ROWS, 512), BF16),
            pltpu.VMEM((2, ROWS, SPAN), jnp.int32),
            pltpu.VMEM((2, KH, ROWS, 128), F32),
            pltpu.VMEM((2, SPAN, 128), F32),
            pltpu.VMEM((2, SPAN, 128), F32),
            pltpu.VMEM((2, ROWS, 128), BF16),
            pltpu.VMEM((SPAN, width), BF16),
            pltpu.VMEM((SPAN, width), BF16),
            pltpu.VMEM((SPAN, width), BF16),
            pltpu.VMEM((NZ, NY, NX, PAD, width), BF16),
            pltpu.VMEM((NZ * NY, NX, PAD, 128), F32),
            pltpu.VMEM((NZ, NX, NY, PAD, 128), F32),
            pltpu.VMEM((14, NX, PAD, 128), F32),
            pltpu.VMEM((6, NY, PAD, 128), F32),
            pltpu.VMEM((NZ * NX - 1, PAD, 128), F32),
            pltpu.VMEM((NZ * NY - 1, PAD, 128), F32),
            pltpu.VMEM((NH, 2, 3, PAD, width), F32),
            pltpu.VMEM((NH, 2, PAD, width), F32),
            pltpu.VMEM((8, 128), F32),
            pltpu.VMEM((NZ * NX - 1, 8, 128), F32),
            pltpu.VMEM((8, 128), F32),
            pltpu.VMEM((NY - 1, 8, 128), F32),
            pltpu.VMEM((NW, 8, 128), F32),
            pltpu.SemaphoreType.DMA((120,)),
            pltpu.SemaphoreType.DMA((120,)),
            pltpu.SemaphoreType.DMA((10,)),
        ],
        compiler_params=pltpu.CompilerParams(
            collective_id=0, has_side_effects=True, vmem_limit_bytes=63 * 1024 * 1024
        ),
        name="local_adam",
    )(
        jnp.swapaxes(inputs[0], 0, 1), queries[0], keys[0], out_grad[0], positions, bands, step,
        *[jnp.swapaxes(a, 0, 1) for a in (value_weight, moment_one, moment_two)], jnp.asarray(spread_matrix(), BF16),
    )
    results = (out, mean_weight, mean_one, mean_two)
    out, mean_weight, mean_one, mean_two = pl.pallas_call(
        hand_over,
        out_shape=tuple(jax.ShapeDtypeStruct(a.shape, a.dtype) for a in results),
        in_specs=[vmem] * 4,
        out_specs=(hbm,) * 4,
        scratch_shapes=[pltpu.SemaphoreType.DMA((4,))],
        name="hand_over",
    )(*results)
    return out[None], mean_weight, mean_one, mean_two


def solution(mesh):
    rows = P("work", "ctx", None)
    in_specs = (rows, rows, rows, rows, P("work", "ctx"), P(), P(), rows, rows, rows)
    out_specs = (rows, P("ctx", None), P("ctx", None), P("ctx", None))
    return jax.shard_map(
        per_device, mesh=mesh, in_specs=in_specs, out_specs=out_specs, check_vma=False
    )
```

```python
import functools
import math

import jax
import jax.numpy as jnp
import numpy as np
from jax import lax
from jax.experimental import pallas as pl
from jax.experimental.pallas import tpu as pltpu
from jax.sharding import PartitionSpec as P

D = 2880
HD = 64
QH = 32
KH = 4
SPAN = 128
ROWS = 256
NZ, NY, NX = 2, 8, 4
NCTX = NZ * NY * NX
NH = 4
NW = 8
OWN = D // NCTX
PAD = 48
HALF = D // NZ
HALF_PAD = NY * NX * PAD
TILES = HALF_PAD // 128

beta_one = 0.9
beta_two = 0.95
adam_eps = 1e-08
learn_rate = 0.01
clip_norm = 0.5

F32 = jnp.float32
BF16 = jnp.bfloat16


def window(tile):
    lane = tile * 128
    source = OWN * (lane // PAD) + min(lane % PAD, OWN - 1)
    low = source // 128 * 128
    return low, min(256, HALF - low)


def spread_matrix():
    out = np.zeros((TILES, 128, 256), np.float32)
    for tile in range(TILES):
        low, width = window(tile)
        for lane in range(128):
            chunk, row = divmod(tile * 128 + lane, PAD)
            if row < OWN:
                at = chunk * OWN + row - low
                assert 0 <= at < width
                out[tile, lane, at] = 1
    return out


def ring_plan(n):
    plan = []
    for way in (1, -1):
        for half in (0, 1):
            far = n // 2 if (way == 1) == (half == 0) else n // 2 - 1
            plan.append((way, half, far))
    return plan


class Ring:
    def __init__(self, n, at, view, landing, send_sem, recv_sem, first_sem, to):
        self.n, self.at, self.view, self.landing = n, at, view, landing
        self.send_sem, self.recv_sem, self.to = send_sem, recv_sem, to
        self.slots = {}
        slot = 0
        for way, half, far in ring_plan(n):
            for step in range(far):
                self.slots[way, half, step] = (slot, first_sem + slot)
                slot += 1
        self.copies = {}

    def step(self, count):
        for longest in (True, False):
            for way, half, far in ring_plan(self.n):
                step = count
                if (far == self.n // 2) != longest or step > far:
                    continue
                left = far - step
                target = lax.rem(self.at + way * left + self.n, self.n)
                mine = self.view(target, half)
                if step > 0:
                    self.copies[way, half, step - 1].wait_recv()
                    slot, _ = self.slots[way, half, step - 1]
                    mine[...] = mine[...] + self.landing.at[slot][...]
                if left > 0:
                    slot, sem = self.slots[way, half, step]
                    copy = pltpu.make_async_remote_copy(
                        src_ref=mine,
                        dst_ref=self.landing.at[slot],
                        send_sem=self.send_sem.at[sem],
                        recv_sem=self.recv_sem.at[sem],
                        device_id=self.to(way),
                        device_id_type=pl.DeviceIdType.MESH,
                    )
                    copy.start()
                    self.copies[way, half, step] = copy

    def finish(self):
        for copy in self.copies.values():
            copy.wait_send()


def kernel(
    acts_hbm, queries_hbm, keys_hbm, out_grad_hbm, positions_hbm, bands, step, weight_hbm, one_hbm, two_hbm, spread_hbm,
    out_hbm, mean_weight, mean_one, mean_two,
    out, acts, queries, keys, out_grad, positions, state, spread, acts_t, k2, v2, probs, dist, dv, dv_send, dv_recv, dv_half, key_halo, value_send, value_halo,
    other_acts, dv_all, part, part_in, whole, gx, gy, rx, ry, rx2, ry2, moments, grads, n_send, n_one, n_two_send, n_two, norms,
    send_sem, recv_sem, load_sem,
):
    ctx = lax.axis_index("ctx")
    wrk = lax.axis_index("work")
    z, y, x = ctx // (NY * NX), lax.rem(ctx // NX, NY), lax.rem(ctx, NX)
    zh, core = wrk // 2, lax.rem(wrk, 2)
    zx = z * NX + x
    nxt = lax.rem(ctx + 1, NCTX)
    prv = lax.rem(ctx + NCTX - 1, NCTX)

    def at_ctx(zz, yy, xx):
        return {"ctx": (zz * NY + yy) * NX + xx}

    def zx_peer(k):
        other = lax.rem(zx + k, NZ * NX)
        return other // NX, lax.rem(other, NX)

    used = [0]
    pending = []

    def send(src, dst, device):
        sem = used[0]
        used[0] += 1
        copy = pltpu.make_async_remote_copy(
            src_ref=src,
            dst_ref=dst,
            send_sem=send_sem.at[sem],
            recv_sem=recv_sem.at[sem],
            device_id=device,
            device_id_type=pl.DeviceIdType.MESH,
        )
        copy.start()
        pending.append(copy)
        return copy

    loads = []
    for index, (source, target) in enumerate((
        (keys_hbm, keys), (positions_hbm, positions), (queries_hbm, queries), (out_grad_hbm, out_grad),
        (weight_hbm, state.at[0]), (one_hbm, state.at[1]), (two_hbm, state.at[2]),
        (spread_hbm, spread), (acts_hbm, acts),
    )):
        load = pltpu.make_async_copy(source, target, load_sem.at[index])
        load.start()
        loads.append(load)

    barrier = pltpu.get_barrier_semaphore()
    greeted = [{"ctx": nxt}, {"ctx": prv}]
    for k in range(1, NZ * NX):
        zz, xx = zx_peer(k)
        greeted.append(at_ctx(zz, y, xx))
    for k in range(1, NY):
        greeted.append(at_ctx(z, lax.rem(y + k, NY), x))
    for k in range(1, NW):
        greeted.append({"work": lax.rem(wrk + k, NW)})
    for device in greeted:
        pl.semaphore_signal(barrier, inc=1, device_id=device, device_id_type=pl.DeviceIdType.MESH)

    low_lane = lax.broadcasted_iota(jnp.int32, (1, 128), 1) < HD

    def widen(source, target, first, count):
        for pair in range(KH // 2):
            tile = source[:, pair * 128 : pair * 128 + 128].astype(F32)
            other = pltpu.roll(tile, HD, 1)
            at = pl.ds(first, count)
            target[2 * pair, 0, at, :] = jnp.where(low_lane, tile, 0.0).astype(BF16)
            target[2 * pair, 1, at, :] = jnp.where(low_lane, 0.0, other).astype(BF16)
            target[2 * pair + 1, 0, at, :] = jnp.where(low_lane, other, 0.0).astype(BF16)
            target[2 * pair + 1, 1, at, :] = jnp.where(low_lane, 0.0, tile).astype(BF16)

    for load in loads[:2]:
        load.wait()
    widen(keys[...], k2, SPAN, ROWS)
    for block in range(2):
        apart = (
            lax.broadcasted_iota(jnp.int32, (ROWS, SPAN), 1)
            + SPAN
            - lax.broadcasted_iota(jnp.int32, (ROWS, SPAN), 0)
        )
        near = (apart >= 0) & (apart <= positions[:, block * SPAN : block * SPAN + SPAN])
        dist[block] = jnp.where(near, apart, 1 << 20)

    factor = HD**-0.5 * math.log2(math.e)

    def attend(pair, block):
        rows = slice(block * SPAN, block * SPAN + SPAN)
        span = slice(block * SPAN, block * SPAN + ROWS)

        def head(index, carry):
            j = 2 * pair + index
            first = pl.multiple_of(j * 512, 512)
            for i in range(4):
                query = queries[rows, pl.ds(pl.multiple_of(first + i * 128, 128), 128)]
                for e in range(2):
                    scores = lax.dot_general(
                        k2[j, e, span, :], query, (((1,), (1,)), ((), ())), preferred_element_type=F32
                    )
                    scores = jnp.where(dist[block] <= bands[j * 8 + 2 * i + e], scores, -1e30)
                    top = jnp.max(scores, axis=0, keepdims=True)
                    expo = jnp.exp2((scores - top) * factor)
                    total = jnp.sum(expo, axis=0, keepdims=True)
                    probs[block, j, e, :, i * 128 : i * 128 + 128] = (expo * (1.0 / total)).astype(BF16)
            cotan = jnp.concatenate(
                [out_grad[rows, pl.ds(pl.multiple_of(first + i * 128, 128), 128)] for i in range(4)], 0
            )
            even = jnp.dot(probs[block, j, 0], cotan, preferred_element_type=F32)
            odd = jnp.dot(probs[block, j, 1], cotan, preferred_element_type=F32)
            dv[block, j] = even + pltpu.roll(odd, HD, 1)
            return carry

        lax.fori_loop(0, 2, head, 0)

    def joined(pair, block):
        return jnp.where(low_lane, dv[block, 2 * pair], pltpu.roll(dv[block, 2 * pair + 1], HD, 1))

    def halo_back(pair):
        dv_send[pair] = joined(pair, 0)[:SPAN]
        return send(dv_send.at[pair], dv_recv.at[pair], {"ctx": prv})

    def value_grad(pair, halo):
        first, second = joined(pair, 0), joined(pair, 1)
        halo.wait_recv()
        dv_half[pair, :SPAN, :] = (first[SPAN:] + second[:SPAN]).astype(BF16)
        dv_half[pair, SPAN:, :] = (second[SPAN:] + dv_recv[pair]).astype(BF16)

    for load in loads[2:4]:
        load.wait()
    attend(0, 1)
    for load in loads[4:7]:
        load.wait()
    spare = jnp.zeros((PAD - OWN, KH * HD), F32)
    for index in range(3):
        moments[zh, core, index] = jnp.concatenate([state[index, :, 0, :], spare], 0)
    whole[y, x] = moments[zh, core, 0].astype(BF16)

    pl.semaphore_wait(barrier, len(greeted))

    keys_in = send(keys.at[pl.ds(ROWS - SPAN, SPAN)], key_halo, {"ctx": nxt})
    loads[8].wait()
    acts_in = send(acts.at[1 - z], other_acts, at_ctx(1 - z, y, x))
    whole_y = [send(whole.at[y, x], whole.at[y, x], at_ctx(z, lax.rem(y + k, NY), x)) for k in range(1, NY)]

    def over_work(buffer):
        far = [
            send(buffer.at[zh, core], buffer.at[zh, core], {"work": lax.rem(zh + k, NH) * 2 + core})
            for k in range(1, NH)
        ]
        near = [send(buffer.at[zh, core], buffer.at[zh, core], {"work": zh * 2 + 1 - core})]

        def forward():
            for k in range(1, NH):
                far[k - 1].wait_recv()
                source = lax.rem(zh + NH - k, NH)
                near.append(
                    send(buffer.at[source, core], buffer.at[source, core], {"work": zh * 2 + 1 - core})
                )

        def arrive():
            for copy in near:
                copy.wait_recv()

        return forward, arrive

    loads[7].wait()

    def spread_out(source, owner):
        def tile_step(low, width, tile):
            at = pl.ds(pl.multiple_of(owner * ROWS, ROWS), ROWS)
            acts_t[tile * 128 : tile * 128 + 128, at] = jnp.dot(
                spread[tile, :, :width], source[low : low + width, :], preferred_element_type=F32
            ).astype(BF16)

        for tile in range(TILES):
            tile_step(*window(tile), tile)

    spread_out(acts.at[z], z)
    attend(1, 1)
    keys_in.wait_recv()
    widen(key_halo[...], k2, 0, SPAN)
    attend(0, 0)
    halo_a = halo_back(0)
    attend(1, 0)
    halo_b = halo_back(1)
    for copy in whole_y:
        copy.wait_recv()
    mine_x = whole.at[:, x]
    whole_x = [send(mine_x, mine_x, at_ctx(z, y, lax.rem(x + k, NX))) for k in range(1, NX)]

    def share(pair):
        at = pl.ds(pl.multiple_of(z * ROWS, ROWS), ROWS)
        dv_all[pair, at, :] = dv_half[pair]
        return send(dv_all.at[pair, at], dv_all.at[pair, at], at_ctx(1 - z, y, x))

    value_grad(0, halo_a)
    shared_a = share(0)
    value_grad(1, halo_b)
    shared_b = share(1)
    acts_in.wait_recv()
    spread_out(other_acts, 1 - z)

    shared_a.wait_recv()
    for i in range(4):
        block = jnp.dot(
            acts_t[i * 384 : i * 384 + 384, :], dv_all[0], preferred_element_type=F32
        ).reshape(2, NX, PAD, 128)
        for t in range(NX):
            gx[t, i // 2, i % 2 * 2 : i % 2 * 2 + 2] = block[:, t]
    ring_x = Ring(
        NX, x, lambda t, h: gx.at[t, h], rx, send_sem, recv_sem, 114,
        lambda way: at_ctx(z, y, lax.rem(x + way + NX, NX)),
    )
    ring_x.step(0)

    shared_b.wait_recv()
    for i in range(2):
        block = jnp.dot(
            acts_t[i * 768 : i * 768 + 768, :], dv_all[1], preferred_element_type=F32
        ).reshape(4, 2, 2, PAD, 128)
        gy[i * 4 : i * 4 + 4] = block
    ring_y = Ring(
        NY, y, lambda t, h: gy.at[t, h], ry, send_sem, recv_sem, 100,
        lambda way: at_ctx(z, lax.rem(y + way + NY, NY), x),
    )
    ring_y.step(0)
    moments_forward, moments_arrive = over_work(moments)
    ring_x.step(1)
    ring_y.step(1)
    for copy in whole_x:
        copy.wait_recv()
    rows_all = whole[...].reshape(HALF_PAD, KH * HD)
    for owner in range(NZ):
        part[owner] = lax.dot_general(
            acts_t[:, owner * ROWS : owner * ROWS + ROWS],
            rows_all,
            (((0,), (0,)), ((), ())),
            preferred_element_type=F32,
        )
    part_copy = send(part.at[1 - z], part_in, at_ctx(1 - z, y, x))
    ring_y.step(2)
    ring_x.step(2)
    second_a = []
    for k in range(1, NY):
        yy = lax.rem(y + k, NY)
        second_a.append(
            send(gx.at[x, yy // 4, lax.rem(yy, 4)], rx2.at[k - 1], at_ctx(z, yy, x))
        )
    ring_y.step(3)
    ring_y.step(4)
    second_b = []
    for k in range(1, NX):
        xx = lax.rem(x + k, NX)
        second_b.append(
            send(gy.at[y, xx // 2, lax.rem(xx, 2)], ry2.at[k - 1], at_ctx(z, y, xx))
        )

    part_copy.wait_recv()
    values = (part[z] + part_in[...]).astype(BF16)
    value_send[...] = values[ROWS - SPAN :]
    values_in = send(value_send, value_halo, {"ctx": nxt})
    widen(values, v2, SPAN, ROWS)

    def output(block):
        rows = slice(block * SPAN, block * SPAN + SPAN)
        span = slice(block * SPAN, block * SPAN + ROWS)

        def head(j, carry):
            total = jnp.zeros((512, 128), F32)
            for e in range(2):
                total += lax.dot_general(
                    probs[block, j, e], v2[j, e, span, :], (((0,), (0,)), ((), ())), preferred_element_type=F32
                )
            for i in range(4):
                out[rows, pl.ds(pl.multiple_of(j * 512 + i * 128, 128), 128)] = total[
                    i * 128 : i * 128 + 128
                ].astype(BF16)
            return carry

        lax.fori_loop(0, KH, head, 0)

    for copy in second_a:
        copy.wait_recv()
    half_a = gx[x, y // 4, lax.rem(y, 4)]
    for k in range(1, NY):
        half_a = half_a + rx2[k - 1]
    for copy in second_b:
        copy.wait_recv()
    half_b = gy[y, x // 2, lax.rem(x, 2)]
    for k in range(1, NX):
        half_b = half_b + ry2[k - 1]
    tokens_all = float(ROWS * NCTX)
    half_a, half_b = half_a / tokens_all, half_b / tokens_all
    grads[zh, core, :, :128] = half_a
    grads[zh, core, :, 128:] = half_b
    grads_forward, grads_arrive = over_work(grads)
    n_send[...] = (half_a * half_a + half_b * half_b).reshape(PAD // 8, 8, 128).sum(0)
    norm_one = []
    for k in range(1, NZ * NX):
        zz, xx = zx_peer(k)
        norm_one.append(send(n_send, n_one.at[k - 1], at_ctx(zz, y, xx)))
    output(1)
    values_in.wait_recv()
    widen(value_halo[...], v2, 0, SPAN)
    for copy in norm_one:
        copy.wait_recv()
    n_two_send[...] = n_send[...] + n_one[...].sum(0)
    norm_two = [
        send(n_two_send, n_two.at[k - 1], at_ctx(z, lax.rem(y + k, NY), x)) for k in range(1, NY)
    ]
    grads_forward()
    moments_forward()
    output(0)
    store = pltpu.make_async_copy(out, out_hbm, load_sem.at[9])
    store.start()
    for copy in norm_two:
        copy.wait_recv()
    norms[wrk] = n_two_send[...] + n_two[...].sum(0)
    norm_work = [
        send(norms.at[wrk], norms.at[wrk], {"work": lax.rem(wrk + k, NW)}) for k in range(1, NW)
    ]
    moments_arrive()
    grads_arrive()
    for copy in norm_work:
        copy.wait_recv()

    count = jnp.full((1, 128), step[0].astype(F32), F32)
    fix_one = (1.0 - jnp.exp(count * math.log(beta_one)))[:, :1]
    fix_two = (1.0 - jnp.exp(count * math.log(beta_two)))[:, :1]
    sums = [jnp.zeros((PAD, KH * HD), F32) for _ in range(3)]
    for w in range(NW):
        square = jnp.sum(jnp.sum(norms[w], axis=0, keepdims=True), axis=1, keepdims=True)
        scale = jnp.minimum(1.0, clip_norm / (jnp.sqrt(square) + 1e-06))
        grad = grads[w // 2, w % 2] * scale
        first = beta_one * moments[w // 2, w % 2, 1] + (1.0 - beta_one) * grad
        second = beta_two * moments[w // 2, w % 2, 2] + (1.0 - beta_two) * grad * grad
        updated = moments[w // 2, w % 2, 0] - learn_rate * (first / fix_one) / (
            jnp.sqrt(second / fix_two) + adam_eps
        )
        sums = [total + part for total, part in zip(sums, (updated, first, second))]
    for target, total in zip((mean_weight, mean_one, mean_two), sums):
        target[...] = (total / NW)[:OWN]

    store.wait()
    for copy in pending:
        copy.wait_send()
    ring_x.finish()
    ring_y.finish()


def hand_over(*refs):
    sems = refs[-1]
    copies = [pltpu.make_async_copy(refs[i], refs[4 + i], sems.at[i]) for i in range(4)]
    for copy in copies:
        copy.start()
    for copy in copies:
        copy.wait()


def per_device(
    inputs, queries, keys, out_grad, positions, bands, step, value_weight, moment_one, moment_two
):
    vmem = pl.BlockSpec(memory_space=pltpu.VMEM)
    hbm = pl.BlockSpec(memory_space=pltpu.HBM)
    smem = pl.BlockSpec(memory_space=pltpu.SMEM)
    width = KH * HD
    out, mean_weight, mean_one, mean_two = pl.pallas_call(
        kernel,
        out_shape=(
            jax.ShapeDtypeStruct((ROWS, QH * HD), BF16),
            *[jax.ShapeDtypeStruct((OWN, width), F32)] * 3,
        ),
        in_specs=[hbm, hbm, hbm, hbm, hbm, smem, smem, hbm, hbm, hbm, hbm],
        out_specs=(hbm, vmem, vmem, vmem),
        scratch_shapes=[
            pltpu.VMEM((ROWS, QH * HD), BF16),
            pltpu.VMEM((NZ, HALF, ROWS), BF16),
            pltpu.VMEM((ROWS, QH * HD), BF16),
            pltpu.VMEM((ROWS, width), BF16),
            pltpu.VMEM((ROWS, QH * HD), BF16),
            pltpu.VMEM((1, ROWS), jnp.int32),
            pltpu.VMEM((3, OWN, 1, width), F32),
            pltpu.VMEM((TILES, 128, 256), BF16),
            pltpu.VMEM((HALF_PAD, NZ * ROWS), BF16),
            pltpu.VMEM((KH, 2, SPAN + ROWS, 128), BF16),
            pltpu.VMEM((KH, 2, SPAN + ROWS, 128), BF16),
            pltpu.VMEM((2, KH, 2, ROWS, 512), BF16),
            pltpu.VMEM((2, ROWS, SPAN), jnp.int32),
            pltpu.VMEM((2, KH, ROWS, 128), F32),
            pltpu.VMEM((2, SPAN, 128), F32),
            pltpu.VMEM((2, SPAN, 128), F32),
            pltpu.VMEM((2, ROWS, 128), BF16),
            pltpu.VMEM((SPAN, width), BF16),
            pltpu.VMEM((SPAN, width), BF16),
            pltpu.VMEM((SPAN, width), BF16),
            pltpu.VMEM((HALF, ROWS), BF16),
            pltpu.VMEM((2, NZ * ROWS, 128), BF16),
            pltpu.VMEM((NZ, ROWS, width), F32),
            pltpu.VMEM((ROWS, width), F32),
            pltpu.VMEM((NY, NX, PAD, width), BF16),
            pltpu.VMEM((NX, 2, NY // 2, PAD, 128), F32),
            pltpu.VMEM((NY, 2, NX // 2, PAD, 128), F32),
            pltpu.VMEM((6, NY // 2, PAD, 128), F32),
            pltpu.VMEM((14, NX // 2, PAD, 128), F32),
            pltpu.VMEM((NY - 1, PAD, 128), F32),
            pltpu.VMEM((NX - 1, PAD, 128), F32),
            pltpu.VMEM((NH, 2, 3, PAD, width), F32),
            pltpu.VMEM((NH, 2, PAD, width), F32),
            pltpu.VMEM((8, 128), F32),
            pltpu.VMEM((NZ * NX - 1, 8, 128), F32),
            pltpu.VMEM((8, 128), F32),
            pltpu.VMEM((NY - 1, 8, 128), F32),
            pltpu.VMEM((NW, 8, 128), F32),
            pltpu.SemaphoreType.DMA((120,)),
            pltpu.SemaphoreType.DMA((120,)),
            pltpu.SemaphoreType.DMA((10,)),
        ],
        compiler_params=pltpu.CompilerParams(
            collective_id=0, has_side_effects=True, vmem_limit_bytes=63 * 1024 * 1024
        ),
        name="local_adam",
    )(
        jnp.swapaxes(inputs[0], 0, 1).reshape(NZ, HALF, ROWS), queries[0], keys[0], out_grad[0], positions, bands, step,
        *[jnp.swapaxes(a, 0, 1) for a in (value_weight, moment_one, moment_two)], jnp.asarray(spread_matrix(), BF16),
    )
    results = (out, mean_weight, mean_one, mean_two)
    out, mean_weight, mean_one, mean_two = pl.pallas_call(
        hand_over,
        out_shape=tuple(jax.ShapeDtypeStruct(a.shape, a.dtype) for a in results),
        in_specs=[vmem] * 4,
        out_specs=(hbm,) * 4,
        scratch_shapes=[pltpu.SemaphoreType.DMA((4,))],
        name="hand_over",
    )(*results)
    return out[None], mean_weight, mean_one, mean_two


def solution(mesh):
    rows = P("work", "ctx", None)
    in_specs = (rows, rows, rows, rows, P("work", "ctx"), P(), P(), rows, rows, rows)
    out_specs = (rows, P("ctx", None), P("ctx", None), P("ctx", None))
    return jax.shard_map(
        per_device, mesh=mesh, in_specs=in_specs, out_specs=out_specs, check_vma=False
    )
```

```python
import functools
import math

import jax
import jax.numpy as jnp
import numpy as np
from jax import lax
from jax.experimental import pallas as pl
from jax.experimental.pallas import tpu as pltpu
from jax.sharding import PartitionSpec as P

D = 2880
HD = 64
QH = 32
KH = 4
SPAN = 128
ROWS = 256
NZ, NY, NX = 2, 8, 4
NCTX = NZ * NY * NX
NH = 4
NW = 8
OWN = D // NCTX
PAD = 48
HALF = D // NZ
HALF_PAD = NY * NX * PAD
TILES = HALF_PAD // 128

beta_one = 0.9
beta_two = 0.95
adam_eps = 1e-08
learn_rate = 0.01
clip_norm = 0.5

F32 = jnp.float32
BF16 = jnp.bfloat16


def window(tile):
    lane = tile * 128
    source = OWN * (lane // PAD) + min(lane % PAD, OWN - 1)
    low = source // 128 * 128
    return low, min(256, HALF - low)


def spread_matrix():
    out = np.zeros((TILES, 128, 256), np.float32)
    for tile in range(TILES):
        low, width = window(tile)
        for lane in range(128):
            chunk, row = divmod(tile * 128 + lane, PAD)
            if row < OWN:
                at = chunk * OWN + row - low
                assert 0 <= at < width
                out[tile, lane, at] = 1
    return out


def ring_plan(n):
    plan = []
    for way in (1, -1):
        for half in (0, 1):
            far = n // 2 if (way == 1) == (half == 0) else n // 2 - 1
            plan.append((way, half, far))
    return plan


class Ring:
    def __init__(self, n, at, view, landing, send_sem, recv_sem, first_sem, to):
        self.n, self.at, self.view, self.landing = n, at, view, landing
        self.send_sem, self.recv_sem, self.to = send_sem, recv_sem, to
        self.slots = {}
        slot = 0
        for way, half, far in ring_plan(n):
            for step in range(far):
                self.slots[way, half, step] = (slot, first_sem + slot)
                slot += 1
        self.copies = {}

    def step(self, count):
        for longest in (True, False):
            for way, half, far in ring_plan(self.n):
                step = count
                if (far == self.n // 2) != longest or step > far:
                    continue
                left = far - step
                target = lax.rem(self.at + way * left + self.n, self.n)
                mine = self.view(target, half)
                if step > 0:
                    self.copies[way, half, step - 1].wait_recv()
                    slot, _ = self.slots[way, half, step - 1]
                    mine[...] = mine[...] + self.landing.at[slot][...]
                if left > 0:
                    slot, sem = self.slots[way, half, step]
                    copy = pltpu.make_async_remote_copy(
                        src_ref=mine,
                        dst_ref=self.landing.at[slot],
                        send_sem=self.send_sem.at[sem],
                        recv_sem=self.recv_sem.at[sem],
                        device_id=self.to(way),
                        device_id_type=pl.DeviceIdType.MESH,
                    )
                    copy.start()
                    self.copies[way, half, step] = copy

    def finish(self):
        for copy in self.copies.values():
            copy.wait_send()


def kernel(
    acts_hbm, queries_hbm, keys_hbm, out_grad_hbm, positions_hbm, bands, step, weight_hbm, one_hbm, two_hbm, spread_hbm,
    out_hbm, mean_weight, mean_one, mean_two,
    out, acts, queries, keys, out_grad, positions, state, spread, acts_t, k2, v2, probs, dist, dv, dv_send, dv_recv, dv_half, key_halo, value_send, value_halo,
    other_acts, dv_all, part, part_in, whole, gx, gy, rx, ry, rx2, ry2, moments, grads, n_send, n_one, n_two_send, n_two, norms,
    send_sem, recv_sem, load_sem,
):
    ctx = lax.axis_index("ctx")
    wrk = lax.axis_index("work")
    z, y, x = ctx // (NY * NX), lax.rem(ctx // NX, NY), lax.rem(ctx, NX)
    zh, core = wrk // 2, lax.rem(wrk, 2)
    zx = z * NX + x
    nxt = lax.rem(ctx + 1, NCTX)
    prv = lax.rem(ctx + NCTX - 1, NCTX)

    def at_ctx(zz, yy, xx):
        return {"ctx": (zz * NY + yy) * NX + xx}

    def zx_peer(k):
        other = lax.rem(zx + k, NZ * NX)
        return other // NX, lax.rem(other, NX)

    used = [0]
    pending = []

    def send(src, dst, device):
        sem = used[0]
        used[0] += 1
        copy = pltpu.make_async_remote_copy(
            src_ref=src,
            dst_ref=dst,
            send_sem=send_sem.at[sem],
            recv_sem=recv_sem.at[sem],
            device_id=device,
            device_id_type=pl.DeviceIdType.MESH,
        )
        copy.start()
        pending.append(copy)
        return copy

    loads = []
    for index, (source, target) in enumerate((
        (keys_hbm, keys), (positions_hbm, positions), (queries_hbm, queries), (out_grad_hbm, out_grad),
        (weight_hbm, state.at[0]), (one_hbm, state.at[1]), (two_hbm, state.at[2]),
        (spread_hbm, spread), (acts_hbm, acts),
    )):
        load = pltpu.make_async_copy(source, target, load_sem.at[index])
        load.start()
        loads.append(load)

    barrier = pltpu.get_barrier_semaphore()
    greeted = [{"ctx": nxt}, {"ctx": prv}]
    for k in range(1, NZ * NX):
        zz, xx = zx_peer(k)
        greeted.append(at_ctx(zz, y, xx))
    for k in range(1, NY):
        greeted.append(at_ctx(z, lax.rem(y + k, NY), x))
    for k in range(1, NW):
        greeted.append({"work": lax.rem(wrk + k, NW)})
    for device in greeted:
        pl.semaphore_signal(barrier, inc=1, device_id=device, device_id_type=pl.DeviceIdType.MESH)

    low_lane = lax.broadcasted_iota(jnp.int32, (1, 128), 1) < HD

    def widen(source, target, first, count):
        for pair in range(KH // 2):
            tile = source[:, pair * 128 : pair * 128 + 128].astype(F32)
            other = pltpu.roll(tile, HD, 1)
            at = pl.ds(first, count)
            target[2 * pair, 0, at, :] = jnp.where(low_lane, tile, 0.0).astype(BF16)
            target[2 * pair, 1, at, :] = jnp.where(low_lane, 0.0, other).astype(BF16)
            target[2 * pair + 1, 0, at, :] = jnp.where(low_lane, other, 0.0).astype(BF16)
            target[2 * pair + 1, 1, at, :] = jnp.where(low_lane, 0.0, tile).astype(BF16)

    for load in loads[:2]:
        load.wait()
    widen(keys[...], k2, SPAN, ROWS)
    for block in range(2):
        apart = (
            lax.broadcasted_iota(jnp.int32, (ROWS, SPAN), 1)
            + SPAN
            - lax.broadcasted_iota(jnp.int32, (ROWS, SPAN), 0)
        )
        near = (apart >= 0) & (apart <= positions[:, block * SPAN : block * SPAN + SPAN])
        dist[block] = jnp.where(near, apart, 1 << 20)

    factor = HD**-0.5 * math.log2(math.e)

    def attend(pair, block):
        rows = slice(block * SPAN, block * SPAN + SPAN)
        span = slice(block * SPAN, block * SPAN + ROWS)

        def head(index, carry):
            j = 2 * pair + index
            first = pl.multiple_of(j * 512, 512)
            for i in range(4):
                query = queries[rows, pl.ds(pl.multiple_of(first + i * 128, 128), 128)]
                for e in range(2):
                    scores = lax.dot_general(
                        k2[j, e, span, :], query, (((1,), (1,)), ((), ())), preferred_element_type=F32
                    )
                    scores = jnp.where(dist[block] <= bands[j * 8 + 2 * i + e], scores, -1e30)
                    top = jnp.max(scores, axis=0, keepdims=True)
                    expo = jnp.exp2((scores - top) * factor)
                    total = jnp.sum(expo, axis=0, keepdims=True)
                    probs[block, j, e, :, i * 128 : i * 128 + 128] = (expo * (1.0 / total)).astype(BF16)
            cotan = jnp.concatenate(
                [out_grad[rows, pl.ds(pl.multiple_of(first + i * 128, 128), 128)] for i in range(4)], 0
            )
            even = jnp.dot(probs[block, j, 0], cotan, preferred_element_type=F32)
            odd = jnp.dot(probs[block, j, 1], cotan, preferred_element_type=F32)
            dv[block, j] = even + pltpu.roll(odd, HD, 1)
            return carry

        lax.fori_loop(0, 2, head, 0)

    def joined(pair, block):
        return jnp.where(low_lane, dv[block, 2 * pair], pltpu.roll(dv[block, 2 * pair + 1], HD, 1))

    def halo_back(pair):
        dv_send[pair] = joined(pair, 0)[:SPAN]
        return send(dv_send.at[pair], dv_recv.at[pair], {"ctx": prv})

    def value_grad(pair, halo):
        first, second = joined(pair, 0), joined(pair, 1)
        halo.wait_recv()
        dv_half[pair, :SPAN, :] = (first[SPAN:] + second[:SPAN]).astype(BF16)
        dv_half[pair, SPAN:, :] = (second[SPAN:] + dv_recv[pair]).astype(BF16)

    pl.semaphore_wait(barrier, len(greeted))

    keys_in = send(keys.at[pl.ds(ROWS - SPAN, SPAN)], key_halo, {"ctx": nxt})
    loads[8].wait()
    acts_in = send(acts.at[1 - z], other_acts, at_ctx(1 - z, y, x))
    for load in loads[2:4]:
        load.wait()
    attend(0, 1)
    for load in loads[4:7]:
        load.wait()
    spare = jnp.zeros((PAD - OWN, KH * HD), F32)
    for index in range(3):
        moments[zh, core, index] = jnp.concatenate([state[index, :, 0, :], spare], 0)
    whole[y, x] = moments[zh, core, 0].astype(BF16)

    whole_y = [send(whole.at[y, x], whole.at[y, x], at_ctx(z, lax.rem(y + k, NY), x)) for k in range(1, NY)]

    def over_work(buffer):
        far = [
            send(buffer.at[zh, core], buffer.at[zh, core], {"work": lax.rem(zh + k, NH) * 2 + core})
            for k in range(1, NH)
        ]
        near = [send(buffer.at[zh, core], buffer.at[zh, core], {"work": zh * 2 + 1 - core})]

        def forward():
            for k in range(1, NH):
                far[k - 1].wait_recv()
                source = lax.rem(zh + NH - k, NH)
                near.append(
                    send(buffer.at[source, core], buffer.at[source, core], {"work": zh * 2 + 1 - core})
                )

        def arrive():
            for copy in near:
                copy.wait_recv()

        return forward, arrive

    loads[7].wait()

    def spread_out(source, owner):
        def tile_step(low, width, tile):
            at = pl.ds(pl.multiple_of(owner * ROWS, ROWS), ROWS)
            acts_t[tile * 128 : tile * 128 + 128, at] = jnp.dot(
                spread[tile, :, :width], source[low : low + width, :], preferred_element_type=F32
            ).astype(BF16)

        for tile in range(TILES):
            tile_step(*window(tile), tile)

    spread_out(acts.at[z], z)
    attend(1, 1)
    keys_in.wait_recv()
    widen(key_halo[...], k2, 0, SPAN)
    attend(0, 0)
    halo_a = halo_back(0)
    attend(1, 0)
    halo_b = halo_back(1)
    for copy in whole_y:
        copy.wait_recv()
    mine_x = whole.at[:, x]
    whole_x = [send(mine_x, mine_x, at_ctx(z, y, lax.rem(x + k, NX))) for k in range(1, NX)]

    def share(pair):
        at = pl.ds(pl.multiple_of(z * ROWS, ROWS), ROWS)
        dv_all[pair, at, :] = dv_half[pair]
        return send(dv_all.at[pair, at], dv_all.at[pair, at], at_ctx(1 - z, y, x))

    value_grad(0, halo_a)
    shared_a = share(0)
    value_grad(1, halo_b)
    shared_b = share(1)
    acts_in.wait_recv()
    spread_out(other_acts, 1 - z)

    shared_a.wait_recv()
    for i in range(4):
        block = jnp.dot(
            acts_t[i * 384 : i * 384 + 384, :], dv_all[0], preferred_element_type=F32
        ).reshape(2, NX, PAD, 128)
        for t in range(NX):
            gx[t, i // 2, i % 2 * 2 : i % 2 * 2 + 2] = block[:, t]
    ring_x = Ring(
        NX, x, lambda t, h: gx.at[t, h], rx, send_sem, recv_sem, 114,
        lambda way: at_ctx(z, y, lax.rem(x + way + NX, NX)),
    )
    ring_x.step(0)

    shared_b.wait_recv()
    for i in range(2):
        block = jnp.dot(
            acts_t[i * 768 : i * 768 + 768, :], dv_all[1], preferred_element_type=F32
        ).reshape(4, 2, 2, PAD, 128)
        gy[i * 4 : i * 4 + 4] = block
    ring_y = Ring(
        NY, y, lambda t, h: gy.at[t, h], ry, send_sem, recv_sem, 100,
        lambda way: at_ctx(z, lax.rem(y + way + NY, NY), x),
    )
    ring_y.step(0)
    moments_forward, moments_arrive = over_work(moments)
    ring_x.step(1)
    ring_y.step(1)
    for copy in whole_x:
        copy.wait_recv()
    rows_all = whole[...].reshape(HALF_PAD, KH * HD)
    for owner in range(NZ):
        part[owner] = lax.dot_general(
            acts_t[:, owner * ROWS : owner * ROWS + ROWS],
            rows_all,
            (((0,), (0,)), ((), ())),
            preferred_element_type=F32,
        )
    part_copy = send(part.at[1 - z], part_in, at_ctx(1 - z, y, x))
    ring_y.step(2)
    ring_x.step(2)
    second_a = []
    for k in range(1, NY):
        yy = lax.rem(y + k, NY)
        second_a.append(
            send(gx.at[x, yy // 4, lax.rem(yy, 4)], rx2.at[k - 1], at_ctx(z, yy, x))
        )
    ring_y.step(3)
    ring_y.step(4)
    second_b = []
    for k in range(1, NX):
        xx = lax.rem(x + k, NX)
        second_b.append(
            send(gy.at[y, xx // 2, lax.rem(xx, 2)], ry2.at[k - 1], at_ctx(z, y, xx))
        )

    part_copy.wait_recv()
    values = (part[z] + part_in[...]).astype(BF16)
    value_send[...] = values[ROWS - SPAN :]
    values_in = send(value_send, value_halo, {"ctx": nxt})
    widen(values, v2, SPAN, ROWS)

    def output(block):
        rows = slice(block * SPAN, block * SPAN + SPAN)
        span = slice(block * SPAN, block * SPAN + ROWS)

        def head(j, carry):
            total = jnp.zeros((512, 128), F32)
            for e in range(2):
                total += lax.dot_general(
                    probs[block, j, e], v2[j, e, span, :], (((0,), (0,)), ((), ())), preferred_element_type=F32
                )
            for i in range(4):
                out[rows, pl.ds(pl.multiple_of(j * 512 + i * 128, 128), 128)] = total[
                    i * 128 : i * 128 + 128
                ].astype(BF16)
            return carry

        lax.fori_loop(0, KH, head, 0)

    for copy in second_a:
        copy.wait_recv()
    half_a = gx[x, y // 4, lax.rem(y, 4)]
    for k in range(1, NY):
        half_a = half_a + rx2[k - 1]
    for copy in second_b:
        copy.wait_recv()
    half_b = gy[y, x // 2, lax.rem(x, 2)]
    for k in range(1, NX):
        half_b = half_b + ry2[k - 1]
    tokens_all = float(ROWS * NCTX)
    half_a, half_b = half_a / tokens_all, half_b / tokens_all
    grads[zh, core, :, :128] = half_a
    grads[zh, core, :, 128:] = half_b
    grads_forward, grads_arrive = over_work(grads)
    n_send[...] = (half_a * half_a + half_b * half_b).reshape(PAD // 8, 8, 128).sum(0)
    norm_one = []
    for k in range(1, NZ * NX):
        zz, xx = zx_peer(k)
        norm_one.append(send(n_send, n_one.at[k - 1], at_ctx(zz, y, xx)))
    output(1)
    values_in.wait_recv()
    widen(value_halo[...], v2, 0, SPAN)
    for copy in norm_one:
        copy.wait_recv()
    n_two_send[...] = n_send[...] + n_one[...].sum(0)
    norm_two = [
        send(n_two_send, n_two.at[k - 1], at_ctx(z, lax.rem(y + k, NY), x)) for k in range(1, NY)
    ]
    grads_forward()
    moments_forward()
    output(0)
    store = pltpu.make_async_copy(out, out_hbm, load_sem.at[9])
    store.start()
    for copy in norm_two:
        copy.wait_recv()
    norms[wrk] = n_two_send[...] + n_two[...].sum(0)
    norm_work = [
        send(norms.at[wrk], norms.at[wrk], {"work": lax.rem(wrk + k, NW)}) for k in range(1, NW)
    ]
    moments_arrive()
    grads_arrive()
    for copy in norm_work:
        copy.wait_recv()

    count = jnp.full((1, 128), step[0].astype(F32), F32)
    fix_one = (1.0 - jnp.exp(count * math.log(beta_one)))[:, :1]
    fix_two = (1.0 - jnp.exp(count * math.log(beta_two)))[:, :1]
    sums = [jnp.zeros((PAD, KH * HD), F32) for _ in range(3)]
    for w in range(NW):
        square = jnp.sum(jnp.sum(norms[w], axis=0, keepdims=True), axis=1, keepdims=True)
        scale = jnp.minimum(1.0, clip_norm / (jnp.sqrt(square) + 1e-06))
        grad = grads[w // 2, w % 2] * scale
        first = beta_one * moments[w // 2, w % 2, 1] + (1.0 - beta_one) * grad
        second = beta_two * moments[w // 2, w % 2, 2] + (1.0 - beta_two) * grad * grad
        updated = moments[w // 2, w % 2, 0] - learn_rate * (first / fix_one) / (
            jnp.sqrt(second / fix_two) + adam_eps
        )
        sums = [total + part for total, part in zip(sums, (updated, first, second))]
    for target, total in zip((mean_weight, mean_one, mean_two), sums):
        target[...] = (total / NW)[:OWN]

    store.wait()
    for copy in pending:
        copy.wait_send()
    ring_x.finish()
    ring_y.finish()


def hand_over(*refs):
    sources, targets, held, load_sem, store_sem = refs[:4], refs[4:8], refs[8:12], refs[12], refs[13]
    rows = ROWS // 4
    parts = [(0, pl.ds(k * rows, rows)) for k in range(4)] + [(n, pl.ds(0, OWN)) for n in (1, 2, 3)]
    loads = [
        pltpu.make_async_copy(sources[n].at[at], held[n].at[at], load_sem.at[k])
        for k, (n, at) in enumerate(parts)
    ]
    stores = [
        pltpu.make_async_copy(held[n].at[at], targets[n].at[at], store_sem.at[k])
        for k, (n, at) in enumerate(parts)
    ]
    for load in loads:
        load.start()
    for load, store in zip(loads, stores):
        load.wait()
        store.start()
    for store in stores:
        store.wait()


def per_device(
    inputs, queries, keys, out_grad, positions, bands, step, value_weight, moment_one, moment_two
):
    vmem = pl.BlockSpec(memory_space=pltpu.VMEM)
    hbm = pl.BlockSpec(memory_space=pltpu.HBM)
    smem = pl.BlockSpec(memory_space=pltpu.SMEM)
    width = KH * HD
    out, mean_weight, mean_one, mean_two = pl.pallas_call(
        kernel,
        out_shape=(
            jax.ShapeDtypeStruct((ROWS, QH * HD), BF16),
            *[jax.ShapeDtypeStruct((OWN, width), F32)] * 3,
        ),
        in_specs=[hbm, hbm, hbm, hbm, hbm, smem, smem, hbm, hbm, hbm, hbm],
        out_specs=(hbm, vmem, vmem, vmem),
        scratch_shapes=[
            pltpu.VMEM((ROWS, QH * HD), BF16),
            pltpu.VMEM((NZ, HALF, ROWS), BF16),
            pltpu.VMEM((ROWS, QH * HD), BF16),
            pltpu.VMEM((ROWS, width), BF16),
            pltpu.VMEM((ROWS, QH * HD), BF16),
            pltpu.VMEM((1, ROWS), jnp.int32),
            pltpu.VMEM((3, OWN, 1, width), F32),
            pltpu.VMEM((TILES, 128, 256), BF16),
            pltpu.VMEM((HALF_PAD, NZ * ROWS), BF16),
            pltpu.VMEM((KH, 2, SPAN + ROWS, 128), BF16),
            pltpu.VMEM((KH, 2, SPAN + ROWS, 128), BF16),
            pltpu.VMEM((2, KH, 2, ROWS, 512), BF16),
            pltpu.VMEM((2, ROWS, SPAN), jnp.int32),
            pltpu.VMEM((2, KH, ROWS, 128), F32),
            pltpu.VMEM((2, SPAN, 128), F32),
            pltpu.VMEM((2, SPAN, 128), F32),
            pltpu.VMEM((2, ROWS, 128), BF16),
            pltpu.VMEM((SPAN, width), BF16),
            pltpu.VMEM((SPAN, width), BF16),
            pltpu.VMEM((SPAN, width), BF16),
            pltpu.VMEM((HALF, ROWS), BF16),
            pltpu.VMEM((2, NZ * ROWS, 128), BF16),
            pltpu.VMEM((NZ, ROWS, width), F32),
            pltpu.VMEM((ROWS, width), F32),
            pltpu.VMEM((NY, NX, PAD, width), BF16),
            pltpu.VMEM((NX, 2, NY // 2, PAD, 128), F32),
            pltpu.VMEM((NY, 2, NX // 2, PAD, 128), F32),
            pltpu.VMEM((6, NY // 2, PAD, 128), F32),
            pltpu.VMEM((14, NX // 2, PAD, 128), F32),
            pltpu.VMEM((NY - 1, PAD, 128), F32),
            pltpu.VMEM((NX - 1, PAD, 128), F32),
            pltpu.VMEM((NH, 2, 3, PAD, width), F32),
            pltpu.VMEM((NH, 2, PAD, width), F32),
            pltpu.VMEM((8, 128), F32),
            pltpu.VMEM((NZ * NX - 1, 8, 128), F32),
            pltpu.VMEM((8, 128), F32),
            pltpu.VMEM((NY - 1, 8, 128), F32),
            pltpu.VMEM((NW, 8, 128), F32),
            pltpu.SemaphoreType.DMA((120,)),
            pltpu.SemaphoreType.DMA((120,)),
            pltpu.SemaphoreType.DMA((10,)),
        ],
        compiler_params=pltpu.CompilerParams(
            collective_id=0, has_side_effects=True, vmem_limit_bytes=63 * 1024 * 1024
        ),
        name="local_adam",
    )(
        jnp.swapaxes(inputs[0], 0, 1).reshape(NZ, HALF, ROWS), queries[0], keys[0], out_grad[0], positions, bands, step,
        *[jnp.swapaxes(a, 0, 1) for a in (value_weight, moment_one, moment_two)], jnp.asarray(spread_matrix(), BF16),
    )
    results = (out, mean_weight, mean_one, mean_two)
    out, mean_weight, mean_one, mean_two = pl.pallas_call(
        hand_over,
        out_shape=tuple(jax.ShapeDtypeStruct(a.shape, a.dtype) for a in results),
        in_specs=[hbm] * 4,
        out_specs=(hbm,) * 4,
        scratch_shapes=[
            *[pltpu.VMEM(a.shape, a.dtype) for a in results],
            pltpu.SemaphoreType.DMA((7,)),
            pltpu.SemaphoreType.DMA((7,)),
        ],
        name="hand_over",
    )(*results)
    return out[None], mean_weight, mean_one, mean_two


def solution(mesh):
    rows = P("work", "ctx", None)
    in_specs = (rows, rows, rows, rows, P("work", "ctx"), P(), P(), rows, rows, rows)
    out_specs = (rows, P("ctx", None), P("ctx", None), P("ctx", None))
    return jax.shard_map(
        per_device, mesh=mesh, in_specs=in_specs, out_specs=out_specs, check_vma=False
    )
```
